256 devices in a mesh: section: 8 (over y, core), tok: 32 (over z, x).
Axes of the slice: x: 4, y: 4, z: 8, core: 2. Of those that a mesh axis runs over, the one named last changes fastest.
Arguments:
- patches: bfloat16 [4096, 6144], P('tok'), may hold values from -6 to 6
- patch_ids: int32 [4096], P('tok'), may hold values from 0 to 255
- pos_table: bfloat16 [256, 6144], replicated, may hold values from -5 to 5
- token_counts: int32 [32], P('tok'), may hold values from 16 to 128, as said below
- norm_gain: float32 [8, 6144], P('section'), may hold values from 0.25 to 1.75
- norm_bias: float32 [8, 6144], P('section'), may hold values from -3 to 3
- branch_scale: float32 [8, 6144], P('section'), may hold values from 0.5 to 2
- act_range: float32 [8, 6144], P('section'), may hold values from 1 to 8
- weight_range: float32 [8, 6144], P('section'), may hold values from 0.125 to 1
- alpha_index: int32 [8], P('section'), may hold values from 2 to 7
Outputs:
- covariance: float32 [8, 128, 6144], P('section')
- channel_mean: float32 [8, 6144], P('section')
The draws below stay inside these ranges and needn't reach their ends.
Inputs may be any that keep to these rules, and one draw needn't show every extreme that they name: Each shard's calibration tokens are its first token_counts slots; at least one shard is full in every draw.
All inputs are finite; a program needn't handle non-finite values.
Results may differ from the reference program's by a relative error of at most 0.0067.
Values may be sent and summed in bfloat16 or wider, within the bound.
A program may use at most 256 MiB of HBM per device.

```python
import math
import jax
import jax.numpy as jnp
from jax import lax

D = 6144
BLOCK = 128
PATCHES = 256
TOK_DEV = 128
TOKENS = 4096
LAYERS = 8
N_TOK = 32


def draw_token_counts(key, part):
    drawn = jax.random.randint(key, (N_TOK,), TOK_DEV // 8, TOK_DEV + 1)
    full_shard = jax.random.randint(jax.random.fold_in(key, 7), (), 0, N_TOK)
    shard_ids = jnp.arange(N_TOK, dtype=jnp.int32)
    return jnp.where(shard_ids == full_shard, TOK_DEV, drawn).astype(jnp.int32)


def place_ends(array, rng, least, largest):
    extent = array.shape
    place = [jax.random.randint(jax.random.fold_in(rng, axis), (), 0, extent[axis]) for axis in range(len(extent))]
    array = array.at[tuple(place)].set(least)
    longest = extent.index(max(extent))
    place[longest] = (place[longest] + 1) % extent[longest]
    return array.at[tuple(place)].set(largest)


def block_scale(key, extent, split, least, top_value):
    level = 1.0
    for position, parts in split:
        draws = jax.random.uniform(jax.random.fold_in(jax.random.fold_in(key, 6), position), (parts,), jnp.float32, least / len(split), top_value / len(split))
        level = level * jnp.repeat(jnp.exp(draws), extent[position] // parts).reshape((-1,) + (1,) * (len(extent) - 1 - position))
    return level


def bell_draw(rng, shape, scale, reach, cuts=(), kind=jnp.bfloat16):
    entries = scale * jax.random.normal(rng, shape, jnp.float32)
    if cuts:
        entries = entries * block_scale(rng, shape, cuts, -0.22, 0.18)
    return jnp.clip(entries, -reach, reach).astype(kind)


def setup_inputs(seed: int = 0) -> dict:
    key_list = jax.random.split(jax.random.key(seed), 11)
    return {
        "patches": bell_draw(key_list[0], (TOKENS, D), 1.0, 6.0, ((0, 32),)),
        "patch_ids": place_ends(jax.random.randint(key_list[1], (TOKENS,), 0, PATCHES), jax.random.fold_in(key_list[1], 1), 0, PATCHES - 1).astype(jnp.int32),
        "pos_table": bell_draw(key_list[2], (PATCHES, D), 0.7, 5.0),
        "token_counts": draw_token_counts(jax.random.fold_in(key_list[10], 71), 0),
        "norm_gain": jnp.clip(1.0 + 0.15 * jax.random.normal(key_list[4], (LAYERS, D), jnp.float32), 0.25, 1.75),
        "norm_bias": bell_draw(key_list[5], (LAYERS, D), 0.5, 3.0, ((0, 8),), jnp.float32),
        "branch_scale": jnp.clip(0.5 + 1.5 * jax.random.uniform(key_list[6], (LAYERS, D), jnp.float32) ** block_scale(key_list[6], (LAYERS, D), ((0, 8),), -0.2, 0.2), 0.5, 2.0),
        "act_range": jnp.clip(jnp.exp(math.log(8.0) - 2.0794415 * jax.random.uniform(key_list[7], (LAYERS, D), jnp.float32) ** block_scale(key_list[7], (LAYERS, D), ((0, 8),), -0.2, 0.2)), 1.0, 8.0),
        "weight_range": jnp.clip(jnp.exp(math.log(1.0) - 2.0794415 * jax.random.uniform(key_list[8], (LAYERS, D), jnp.float32) ** block_scale(key_list[8], (LAYERS, D), ((0, 8),), -0.2, 0.2)), 0.125, 1.0),
        "alpha_index": place_ends(jax.random.randint(key_list[9], (LAYERS,), 2, 8), jax.random.fold_in(key_list[9], 1), 2, 7).astype(jnp.int32),
    }


def layer_norm(values, gain, bias_row):
    centre = lax.optimization_barrier(jnp.mean(values, axis=-1, keepdims=True))
    spread = lax.optimization_barrier(jnp.mean(jnp.square(values - centre), axis=-1, keepdims=True))
    return (values - centre) * lax.rsqrt(spread + 1e-06) * gain + bias_row

def smoothing(act_row, weight_row, alpha_code):
    exponent = alpha_code.astype(jnp.float32) / 8.0
    return jnp.exp(exponent * jnp.log(act_row) + (exponent - 1.0) * jnp.log(weight_row))

def reference(patches, patch_ids, pos_table, token_counts, norm_gain, norm_bias, branch_scale, act_range, weight_range, alpha_index):
    looked_up = jnp.take(pos_table, patch_ids, axis=0).astype(jnp.float32)
    hidden = (patches.astype(jnp.float32) + looked_up).astype(jnp.bfloat16)
    positions = jnp.arange(TOK_DEV, dtype=jnp.int32)
    valid_rows = (positions[None, :] < token_counts[:, None]).reshape(TOKENS).astype(jnp.float32)
    tokens_used = jnp.sum(valid_rows)
    cov_list = []
    mean_list = []
    for layer_idx in range(LAYERS):
        normed = layer_norm(hidden.astype(jnp.float32), norm_gain[layer_idx], norm_bias[layer_idx])
        factor = smoothing(act_range[layer_idx], weight_range[layer_idx], alpha_index[layer_idx])
        smoothed = (normed / factor).astype(jnp.bfloat16)
        weighted = smoothed.astype(jnp.float32) * valid_rows[:, None]
        mean_row = lax.optimization_barrier(jnp.sum(weighted, axis=0)) / tokens_used
        centred = (smoothed.astype(jnp.float32) - mean_row[None, :]) * valid_rows[:, None]
        gram_block = jnp.dot(centred[:, :BLOCK].T, centred, precision=lax.Precision.HIGHEST, preferred_element_type=jnp.float32)
        cov_list.append(gram_block / tokens_used)
        mean_list.append(mean_row)
        hidden = (hidden.astype(jnp.float32) + branch_scale[layer_idx] * jax.nn.gelu(normed)).astype(jnp.bfloat16)
    return (jnp.stack(cov_list), jnp.stack(mean_list))
```

```python
import functools

import jax
import jax.numpy as jnp
from jax import lax
from jax.experimental import pallas as pl
from jax.experimental.pallas import tpu as pltpu
from jax.sharding import PartitionSpec as P

BLOCK = 128
RING_X = 4
STEP = 512
F32 = jnp.float32
BF16 = jnp.bfloat16
MESH = pl.DeviceIdType.MESH
CONTRACT_ROWS = (((0,), (0,)), ((), ()))


def columns(c, size=STEP):
    return pl.ds(pl.multiple_of(c * size, size), size)


def fold_lanes(values):
    total = values[:, :128]
    for k in range(1, values.shape[1] // 128):
        total = total + values[:, k * 128:(k + 1) * 128]
    return total


def kernel(
    sections,
    toks,
    ids,
    count,
    alpha,
    patches,
    table,
    gain,
    bias,
    scale,
    act,
    weight,
    out_cov,
    out_mean,
    own_patches,
    table_here,
    ranges,
    params,
    hidden,
    smooth,
    tokens,
    gram,
    mean_send,
    gram_x,
    mean_x,
    part_z,
    mean_z_send,
    gram_z,
    mean_z,
    spread,
    slab,
    full,
    mean_full,
    load_sem,
    par_send,
    par_recv,
    smo_send,
    smo_recv,
    rsx_send,
    rsx_recv,
    rmx_send,
    rmx_recv,
    rsz_send,
    rsz_recv,
    rmz_send,
    rmz_recv,
    agz_send,
    agz_recv,
    agx_send,
    agx_recv,
    agm_send,
    agm_recv,
    store_sem,
):
    s = lax.axis_index("section")
    t = lax.axis_index("tok")
    nx = RING_X
    nz = toks // nx
    x = lax.rem(t, nx)
    z = lax.div(t, nx)
    width = patches.shape[1]
    rows = patches.shape[0] // sections
    wide = width // nx
    slim = BLOCK // nz
    steps = width // STEP

    def to_section(other):
        return {"section": other, "tok": t}

    def to_x(other):
        return {"section": s, "tok": z * nx + other}

    def to_z(other):
        return {"section": s, "tok": other * nx + x}

    def others(size, me, fn):
        def go(k, _):
            fn(lax.rem(me + k, size))
            return 0

        lax.fori_loop(1, size, go, 0)

    loads = [
        pltpu.make_async_copy(act, ranges.at[0], load_sem.at[0]),
        pltpu.make_async_copy(weight, ranges.at[1], load_sem.at[1]),
        pltpu.make_async_copy(gain, params.at[s, 0], load_sem.at[2]),
        pltpu.make_async_copy(bias, params.at[s, 1], load_sem.at[3]),
        pltpu.make_async_copy(scale, params.at[s, 2], load_sem.at[4]),
        pltpu.make_async_copy(
            patches.at[pl.ds(pl.multiple_of(s * rows, rows), rows)], own_patches, load_sem.at[5]
        ),
        pltpu.make_async_copy(table, table_here, load_sem.at[6]),
    ]
    for load in loads:
        load.start()

    barrier = pltpu.get_barrier_semaphore()

    def greet(where):
        pl.semaphore_signal(barrier, inc=1, device_id=where, device_id_type=MESH)

    others(sections, s, lambda k: greet(to_section(k)))
    others(nx, x, lambda k: greet(to_x(k)))
    others(nz, z, lambda k: greet(to_z(k)))

    loads[0].wait()
    loads[1].wait()
    exponent = jnp.full((1, STEP), alpha[0], jnp.int32).astype(F32) / 8.0

    def factor_step(c, _):
        cols = columns(c)
        log_factor = exponent * jnp.log(ranges[0, :, cols]) + (exponent - 1.0) * jnp.log(
            ranges[1, :, cols]
        )
        params[s, 3, :, cols] = jnp.exp(-log_factor)
        return 0

    lax.fori_loop(0, steps, factor_step, 0)
    for load in loads[2:5]:
        load.wait()
    pl.semaphore_wait(barrier, sections - 1 + nx - 1 + nz - 1)

    def params_copy(layer, other):
        return pltpu.make_async_remote_copy(
            src_ref=params.at[layer],
            dst_ref=params.at[layer],
            send_sem=par_send.at[other],
            recv_sem=par_recv.at[layer],
            device_id=to_section(other),
            device_id_type=MESH,
        )

    others(sections, s, lambda k: params_copy(s, k).start())

    loads[5].wait()
    loads[6].wait()
    patch = lax.broadcasted_iota(jnp.int32, (rows, table.shape[0]), 1)
    row = lax.broadcasted_iota(jnp.int32, (rows, table.shape[0]), 0)
    wanted = jnp.zeros((rows, table.shape[0]), jnp.int32)
    for r in range(rows):
        wanted = jnp.where(row == r, ids[s * rows + r], wanted)
    pick = (patch == wanted).astype(F32).astype(BF16)

    def start_step(c, total):
        cols = columns(c)
        looked_up = jnp.dot(pick, table_here[:, cols], preferred_element_type=F32)
        first = (own_patches[:, cols].astype(F32) + looked_up).astype(BF16).astype(F32)
        hidden[:, cols] = first
        return total + fold_lanes(first)

    no_total = jnp.zeros((rows, 128), F32)
    first_total = lax.fori_loop(0, steps, start_step, no_total)

    def smooth_copy(layer, source):
        return pltpu.make_async_remote_copy(
            src_ref=smooth.at[layer],
            dst_ref=tokens.at[source],
            send_sem=smo_send.at[layer],
            recv_sem=smo_recv.at[source],
            device_id=to_section(layer),
            device_id_type=MESH,
        )

    def layer_step(layer, total):
        @pl.when(layer != s)
        def _():
            params_copy(layer, s).wait_recv()

        centre = jnp.sum(total, axis=1, keepdims=True) * (1.0 / width)

        def spread_step(c, squares):
            away = hidden[:, columns(c)] - centre
            return squares + fold_lanes(away * away)

        squares = lax.fori_loop(0, steps, spread_step, no_total)
        variance = jnp.sum(squares, axis=1, keepdims=True) * (1.0 / width)
        inverse = lax.rsqrt(variance + 1e-06)

        def value_step(c, new_total):
            cols = columns(c)
            current = hidden[:, cols]
            normed = (current - centre) * inverse * params[layer, 0, :, cols] + params[
                layer, 1, :, cols
            ]
            smooth[layer, :, cols] = (normed * params[layer, 3, :, cols]).astype(BF16)
            inner = normed * (0.7978845608028654 + 0.035677408136300125 * (normed * normed))
            branch = 0.5 * normed * (1.0 + jnp.tanh(inner))
            updated = (current + params[layer, 2, :, cols] * branch).astype(BF16).astype(F32)
            hidden[:, cols] = updated
            return new_total + fold_lanes(updated)

        new_total = lax.fori_loop(0, steps, value_step, no_total)

        @pl.when(layer != s)
        def _():
            smooth_copy(layer, s).start()

        return new_total

    lax.fori_loop(0, sections, layer_step, first_total)
    tokens[s] = smooth[s]
    others(sections, s, lambda k: smooth_copy(s, k).wait_recv())

    shard_rows = sections * rows
    used = jnp.full((1, 128), count[0], jnp.int32)
    used_f = used.astype(F32)
    position = lax.broadcasted_iota(jnp.int32, (shard_rows, 128), 0)
    valid = (position < count[0]).astype(F32).astype(BF16)
    across = lax.broadcasted_iota(jnp.int32, (16, shard_rows), 1)
    valid_row = (across < count[0]).astype(F32).astype(BF16)
    block = tokens[:, :, :BLOCK].reshape(shard_rows, BLOCK) * valid
    block_sum = lax.dot_general(block, valid, CONTRACT_ROWS, preferred_element_type=F32)
    share = 1.0 / used_f[:, :1]

    def gram_step(c, _):
        cols = columns(c)
        here = tokens[:, :, cols].reshape(shard_rows, STEP)
        mean_here = jnp.dot(valid_row, here, preferred_element_type=F32)[:1] * share
        moments = lax.dot_general(block, here, CONTRACT_ROWS, preferred_element_type=F32)
        gram[:, cols] = (moments - block_sum[:, :1] * mean_here).astype(BF16)
        mean_full[:, cols] = mean_here
        return 0

    lax.fori_loop(0, steps, gram_step, 0)
    for k in range(nx):
        mean_send[k, :, :wide] = mean_full[:, k * wide:(k + 1) * wide]
        mean_send[k, :, wide:wide + BLOCK] = mean_full[:, :BLOCK]
        mean_send[k, :, wide + BLOCK:] = used_f

    def wide_cols(k):
        return pl.ds(pl.multiple_of(k * wide, wide), wide)

    def rsx(target, source):
        return (
            pltpu.make_async_remote_copy(
                src_ref=gram.at[:, wide_cols(target)],
                dst_ref=gram_x.at[source],
                send_sem=rsx_send.at[target],
                recv_sem=rsx_recv.at[source],
                device_id=to_x(target),
                device_id_type=MESH,
            ),
            pltpu.make_async_remote_copy(
                src_ref=mean_send.at[target],
                dst_ref=mean_x.at[source],
                send_sem=rmx_send.at[target],
                recv_sem=rmx_recv.at[source],
                device_id=to_x(target),
                device_id_type=MESH,
            ),
        )

    def start_both(pair):
        pair[0].start()
        pair[1].start()

    def recv_both(pair):
        pair[0].wait_recv()
        pair[1].wait_recv()

    others(nx, x, lambda k: start_both(rsx(k, x)))
    mean_x[x] = mean_send[x]
    others(nx, x, lambda k: recv_both(rsx(x, k)))

    def merge_means(means, size):
        rows_of = [means[k] for k in range(size)]
        counts = [one[:, wide + BLOCK:wide + BLOCK + 1] for one in rows_of]
        joined = functools.reduce(jnp.add, counts)
        middle = functools.reduce(
            jnp.add, [one[:, :wide + BLOCK] * n for one, n in zip(rows_of, counts)]
        ) / joined
        index = lax.broadcasted_iota(jnp.int32, (8, wide + BLOCK), 0)
        away = jnp.zeros((8, wide + BLOCK), F32)
        weight_of = jnp.zeros((8, 1), F32)
        index_one = lax.broadcasted_iota(jnp.int32, (8, 1), 0)
        for k in range(size):
            away = jnp.where(index == k, rows_of[k][:, :wide + BLOCK] - middle, away)
            weight_of = jnp.where(index_one == k, counts[k], weight_of)
        pushed = away[:, wide:] * weight_of
        spread[...] = lax.dot_general(
            pushed, away[:, :wide], CONTRACT_ROWS,
            precision=lax.Precision.HIGHEST, preferred_element_type=F32,
        )
        return joined, middle

    joined_x, middle_x = merge_means(mean_x, nx)
    mean_z_send[:, :wide + BLOCK] = middle_x
    mean_z_send[:, wide + BLOCK:] = jnp.broadcast_to(joined_x, (1, BLOCK))

    def join_x(k, _):
        here = pl.ds(pl.multiple_of(k * slim, slim), slim)
        total = spread[here, :] + gram[here, wide_cols(x)].astype(F32)
        for j in range(1, nx):
            total = total + gram_x[lax.rem(x + j, nx), here, :].astype(F32)
        part_z[k] = total.astype(BF16)
        return 0

    lax.fori_loop(0, nz, join_x, 0)

    def rsz(target, source):
        return (
            pltpu.make_async_remote_copy(
                src_ref=part_z.at[target],
                dst_ref=gram_z.at[source],
                send_sem=rsz_send.at[target],
                recv_sem=rsz_recv.at[source],
                device_id=to_z(target),
                device_id_type=MESH,
            ),
            pltpu.make_async_remote_copy(
                src_ref=mean_z_send,
                dst_ref=mean_z.at[source],
                send_sem=rmz_send.at[target],
                recv_sem=rmz_recv.at[source],
                device_id=to_z(target),
                device_id_type=MESH,
            ),
        )

    others(nz, z, lambda k: start_both(rsz(k, z)))
    mean_z[z] = mean_z_send[...]
    gram_z[z] = part_z[z]
    others(nz, z, lambda k: recv_both(rsz(z, k)))

    joined_z, middle_z = merge_means(mean_z, nz)
    total = spread[pl.ds(pl.multiple_of(z * slim, slim), slim), :]
    for k in range(nz):
        total = total + gram_z[k].astype(F32)
    slab[z] = (total / joined_z).astype(BF16)
    mean_full[:, wide_cols(x)] = middle_z[:, :wide]

    def agz(target, source):
        return pltpu.make_async_remote_copy(
            src_ref=slab.at[source],
            dst_ref=slab.at[source],
            send_sem=agz_send.at[target],
            recv_sem=agz_recv.at[source],
            device_id=to_z(target),
            device_id_type=MESH,
        )

    def agm(target, source):
        return pltpu.make_async_remote_copy(
            src_ref=mean_full.at[:, wide_cols(source)],
            dst_ref=mean_full.at[:, wide_cols(source)],
            send_sem=agm_send.at[target],
            recv_sem=agm_recv.at[source],
            device_id=to_x(target),
            device_id_type=MESH,
        )

    others(nz, z, lambda k: agz(k, z).start())
    others(nx, x, lambda k: agm(k, x).start())
    others(nz, z, lambda k: agz(z, k).wait_recv())

    def agx(target, source):
        return pltpu.make_async_remote_copy(
            src_ref=slab,
            dst_ref=full.at[source],
            send_sem=agx_send.at[target],
            recv_sem=agx_recv.at[source],
            device_id=to_x(target),
            device_id_type=MESH,
        )

    others(nx, x, lambda k: agx(k, x).start())
    full[x] = slab[...]

    def store(source):
        return pltpu.make_async_copy(full.at[source], out_cov.at[source], store_sem.at[source])

    store(x).start()
    others(nx, x, lambda k: agm(x, k).wait_recv())
    mean_store = pltpu.make_async_copy(mean_full, out_mean, store_sem.at[nx])
    mean_store.start()

    def arrived(k):
        agx(x, k).wait_recv()
        store(k).start()

    others(nx, x, arrived)

    others(sections, s, lambda k: params_copy(s, k).wait_send())
    others(sections, s, lambda k: smooth_copy(k, s).wait_send())
    others(nx, x, lambda k: rsx(k, x)[0].wait_send())
    others(nx, x, lambda k: rsx(k, x)[1].wait_send())
    others(nz, z, lambda k: rsz(k, z)[0].wait_send())
    others(nz, z, lambda k: rsz(k, z)[1].wait_send())
    others(nz, z, lambda k: agz(k, z).wait_send())
    others(nx, x, lambda k: agm(k, x).wait_send())
    others(nx, x, lambda k: agx(k, x).wait_send())
    mean_store.wait()
    for k in range(nx):
        store(k).wait()


def body(
    patches, patch_ids, pos_table, token_counts, norm_gain, norm_bias, branch_scale, act_range,
    weight_range, alpha_index,
):
    sections = lax.axis_size("section")
    toks = lax.axis_size("tok")
    nx, nz = RING_X, toks // RING_X
    width = patches.shape[1]
    rows = patches.shape[0] // sections
    wide = width // nx
    slim = BLOCK // nz
    meta = wide + 2 * BLOCK
    dma = pltpu.SemaphoreType.DMA
    smem = pl.BlockSpec(memory_space=pltpu.SMEM)
    hbm = pl.BlockSpec(memory_space=pl.ANY)
    vmem = pltpu.VMEM
    cov, mean = pl.pallas_call(
        functools.partial(kernel, sections, toks),
        out_shape=(
            jax.ShapeDtypeStruct((nx, nz, slim, wide), BF16),
            jax.ShapeDtypeStruct((1, width), F32),
        ),
        in_specs=[smem] * 3 + [hbm] * 7,
        out_specs=(hbm, hbm),
        scratch_shapes=[
            vmem((rows, width), BF16),
            vmem(pos_table.shape, BF16),
            vmem((2, 1, width), F32),
            vmem((sections, 4, 1, width), F32),
            vmem((rows, width), F32),
            vmem((sections, rows, width), BF16),
            vmem((sections, rows, width), BF16),
            vmem((BLOCK, width), BF16),
            vmem((nx, 1, meta), F32),
            vmem((nx, BLOCK, wide), BF16),
            vmem((nx, 1, meta), F32),
            vmem((nz, slim, wide), BF16),
            vmem((1, meta), F32),
            vmem((nz, slim, wide), BF16),
            vmem((nz, 1, meta), F32),
            vmem((BLOCK, wide), F32),
            vmem((nz, slim, wide), BF16),
            vmem((nx, nz, slim, wide), BF16),
            vmem((1, width), F32),
            dma((7,)),
            dma((sections,)),
            dma((sections,)),
            dma((sections,)),
            dma((sections,)),
            dma((nx,)),
            dma((nx,)),
            dma((nx,)),
            dma((nx,)),
            dma((nz,)),
            dma((nz,)),
            dma((nz,)),
            dma((nz,)),
            dma((nz,)),
            dma((nz,)),
            dma((nx,)),
            dma((nx,)),
            dma((nx,)),
            dma((nx,)),
            dma((nx + 1,)),
        ],
        compiler_params=pltpu.CompilerParams(
            collective_id=0, has_side_effects=True, vmem_limit_bytes=40 * 1024 * 1024
        ),
        name="moments",
    )(
        patch_ids, token_counts, alpha_index, patches, pos_table, norm_gain, norm_bias,
        branch_scale, act_range, weight_range,
    )
    cov = cov.reshape(nx, BLOCK, wide).transpose(1, 0, 2).reshape(1, BLOCK, width)
    return cov.astype(F32), mean


def solution(mesh):
    in_specs = (
        P("tok", None),
        P("tok"),
        P(),
        P("tok"),
        P("section", None),
        P("section", None),
        P("section", None),
        P("section", None),
        P("section", None),
        P("section"),
    )
    out_specs = (P("section", None, None), P("section", None))
    return jax.shard_map(body, mesh=mesh, in_specs=in_specs, out_specs=out_specs, check_vma=False)
```

```python
import functools

import jax
import jax.numpy as jnp
from jax import lax
from jax.experimental import pallas as pl
from jax.experimental.pallas import tpu as pltpu
from jax.sharding import PartitionSpec as P

BLOCK = 128
RING_X = 4
STEP = 512
CHUNKS = 4
EARLY = 1
F32 = jnp.float32
BF16 = jnp.bfloat16
MESH = pl.DeviceIdType.MESH
CONTRACT_ROWS = (((0,), (0,)), ((), ()))


def columns(c, size=STEP):
    return pl.ds(pl.multiple_of(c * size, size), size)


def fold_lanes(values):
    total = values[:, :128]
    for k in range(1, values.shape[1] // 128):
        total = total + values[:, k * 128:(k + 1) * 128]
    return total


def others(size, me, fn):
    def go(k, _):
        fn(lax.rem(me + k, size))
        return 0

    lax.fori_loop(1, size, go, 0)


def merge_means(means, size, wide, spread):
    rows_of = [means[k] for k in range(size)]
    counts = [one[:, wide + BLOCK:wide + BLOCK + 1] for one in rows_of]
    joined = functools.reduce(jnp.add, counts)
    middle = functools.reduce(
        jnp.add, [one[:, :wide + BLOCK] * n for one, n in zip(rows_of, counts)]
    ) / joined
    index = lax.broadcasted_iota(jnp.int32, (8, wide + BLOCK), 0)
    away = jnp.zeros((8, wide + BLOCK), F32)
    weight_of = jnp.zeros((8, 1), F32)
    index_one = lax.broadcasted_iota(jnp.int32, (8, 1), 0)
    for k in range(size):
        away = jnp.where(index == k, rows_of[k][:, :wide + BLOCK] - middle, away)
        weight_of = jnp.where(index_one == k, counts[k], weight_of)
    pushed = away[:, wide:] * weight_of
    spread[...] = lax.dot_general(
        pushed, away[:, :wide], CONTRACT_ROWS,
        precision=lax.Precision.HIGHEST, preferred_element_type=F32,
    )
    return joined, middle


def kernel(
    sections, toks, ids, count, alpha, patches, table, gain, bias, scale, act, weight, out_cov,
    out_mean, own_patches, table_here, ranges, params, hidden, smooth, tokens, gram, mean_send,
    gram_x, mean_x, part_z, mean_z_send, gram_z, mean_z, spread, slab, full, mean_part, mean_full,
    load_sem, par_send, par_pass, par_recv, smo_send, smo_recv, rsx_send, rsx_recv, rmx_send,
    rmx_recv, rsz_send, rsz_recv, rmz_send, rmz_recv, agz_send, agz_recv, agx_send, agx_recv,
    agm_send, agm_recv, store_sem, mean_sem,
):
    s = lax.axis_index("section")
    t = lax.axis_index("tok")
    ny = sections // 2
    nx = RING_X
    nz = toks // nx
    y = lax.div(s, 2)
    core = lax.rem(s, 2)
    partner = s + 1 - 2 * core
    x = lax.rem(t, nx)
    z = lax.div(t, nx)
    width = patches.shape[1]
    rows = patches.shape[0] // sections
    part = width // CHUNKS
    wide = part // nx
    slim = BLOCK // nz
    steps = width // STEP

    def to_section(other):
        return {"section": other, "tok": t}

    def to_x(other):
        return {"section": s, "tok": z * nx + other}

    def to_z(other):
        return {"section": s, "tok": other * nx + x}

    def remote(src, dst, send, recv, where):
        return pltpu.make_async_remote_copy(
            src_ref=src, dst_ref=dst, send_sem=send, recv_sem=recv, device_id=where,
            device_id_type=MESH,
        )

    loads = [
        pltpu.make_async_copy(act, ranges.at[0], load_sem.at[0]),
        pltpu.make_async_copy(weight, ranges.at[1], load_sem.at[1]),
        pltpu.make_async_copy(gain, params.at[s, 0], load_sem.at[2]),
        pltpu.make_async_copy(bias, params.at[s, 1], load_sem.at[3]),
        pltpu.make_async_copy(scale, params.at[s, 2], load_sem.at[4]),
        pltpu.make_async_copy(
            patches.at[pl.ds(pl.multiple_of(s * rows, rows), rows)], own_patches, load_sem.at[5]
        ),
        pltpu.make_async_copy(table, table_here, load_sem.at[6]),
    ]
    for load in loads:
        load.start()

    barrier = pltpu.get_barrier_semaphore()

    def greet(where):
        pl.semaphore_signal(barrier, inc=1, device_id=where, device_id_type=MESH)

    others(sections, s, lambda k: greet(to_section(k)))
    others(nx, x, lambda k: greet(to_x(k)))
    others(nz, z, lambda k: greet(to_z(k)))

    loads[0].wait()
    loads[1].wait()
    exponent = jnp.full((1, STEP), alpha[0], jnp.int32).astype(F32) / 8.0

    def factor_step(c, _):
        cols = columns(c)
        log_factor = exponent * jnp.log(ranges[0, :, cols]) + (exponent - 1.0) * jnp.log(
            ranges[1, :, cols]
        )
        params[s, 3, :, cols] = jnp.exp(-log_factor)
        return 0

    lax.fori_loop(0, steps, factor_step, 0)
    for load in loads[2:5]:
        load.wait()
    pl.semaphore_wait(barrier, sections - 1 + nx - 1 + nz - 1)

    def params_copy(layer, other, send):
        return remote(
            params.at[layer], params.at[layer], send, par_recv.at[layer], to_section(other)
        )

    def params_across(k):
        return params_copy(s, 2 * k + core, par_send.at[k])

    def params_over():
        return params_copy(s, partner, par_send.at[y])

    def params_on(layer):
        return params_copy(layer, partner, par_pass.at[lax.div(layer, 2)])

    others(ny, y, lambda k: params_across(k).start())
    params_over().start()

    def pass_on(layer):
        @pl.when(jnp.logical_and(layer < sections, layer != s))
        def _():
            params_on(layer).wait_recv()
            params_on(layer).start()

    loads[5].wait()
    loads[6].wait()
    patch = lax.broadcasted_iota(jnp.int32, (rows, table.shape[0]), 1)
    row = lax.broadcasted_iota(jnp.int32, (rows, table.shape[0]), 0)
    wanted = jnp.zeros((rows, table.shape[0]), jnp.int32)
    for r in range(rows):
        wanted = jnp.where(row == r, ids[s * rows + r], wanted)
    pick = (patch == wanted).astype(F32).astype(BF16)

    def start_step(c, total):
        cols = columns(c)
        looked_up = jnp.dot(pick, table_here[:, cols], preferred_element_type=F32)
        first = (own_patches[:, cols].astype(F32) + looked_up).astype(BF16).astype(F32)
        hidden[:, cols] = first
        return total + fold_lanes(first)

    no_total = jnp.zeros((rows, 128), F32)
    first_total = lax.fori_loop(0, steps, start_step, no_total)
    pass_on(core)

    def smooth_copy(c, layer, source):
        return remote(
            smooth.at[c, layer], tokens.at[c, source], smo_send.at[c, layer],
            smo_recv.at[c, source], to_section(layer),
        )

    def layer_step(layer, total):
        mine = lax.rem(layer, 2) == core

        @pl.when(mine)
        def _():
            pass_on(layer + 2)

        @pl.when(jnp.logical_not(mine))
        def _():
            params_on(layer).wait_recv()

        centre = jnp.sum(total, axis=1, keepdims=True) * (1.0 / width)

        def spread_step(c, squares):
            away = hidden[:, columns(c)] - centre
            return squares + fold_lanes(away * away)

        squares = lax.fori_loop(0, steps, spread_step, no_total)
        variance = jnp.sum(squares, axis=1, keepdims=True) * (1.0 / width)
        inverse = lax.rsqrt(variance + 1e-06)
        new_total = no_total
        for c in range(CHUNKS):

            def value_step(k, so_far, c=c):
                cols = pl.ds(pl.multiple_of(c * part + k * STEP, STEP), STEP)
                current = hidden[:, cols]
                normed = (current - centre) * inverse * params[layer, 0, :, cols] + params[
                    layer, 1, :, cols
                ]
                smooth[c, layer, :, columns(k)] = (normed * params[layer, 3, :, cols]).astype(BF16)
                inner = normed * (
                    0.7978845608028654 + 0.035677408136300125 * (normed * normed)
                )
                branch = 0.5 * normed * (1.0 + jnp.tanh(inner))
                updated = (current + params[layer, 2, :, cols] * branch).astype(BF16).astype(F32)
                hidden[:, cols] = updated
                return so_far + fold_lanes(updated)

            new_total = lax.fori_loop(0, part // STEP, value_step, new_total)
            if c < EARLY:

                @pl.when(layer != s)
                def _(c=c):
                    smooth_copy(c, layer, s).start()

        return new_total

    lax.fori_loop(0, sections, layer_step, first_total)
    for c in range(CHUNKS):
        if c >= EARLY:
            others(sections, s, lambda k: smooth_copy(c, k, s).start())
        tokens[c, s] = smooth[c, s]

    shard_rows = sections * rows
    used = jnp.full((1, 128), count[0], jnp.int32).astype(F32)
    share = 1.0 / used[:, :1]
    position = lax.broadcasted_iota(jnp.int32, (shard_rows, 128), 0)
    valid = (position < count[0]).astype(F32).astype(BF16)
    across = lax.broadcasted_iota(jnp.int32, (16, shard_rows), 1)
    valid_row = (across < count[0]).astype(F32).astype(BF16)
    kept = {}

    def rsx(c, target, source):
        where = to_x(target)
        return (
            remote(gram.at[c, target], gram_x.at[c, source], rsx_send.at[c, target],
                   rsx_recv.at[c, source], where),
            remote(mean_send.at[c, target], mean_x.at[c, source], rmx_send.at[c, target],
                   rmx_recv.at[c, source], where),
        )

    def rsz(c, target, source):
        where = to_z(target)
        return (
            remote(part_z.at[c, target], gram_z.at[c, source], rsz_send.at[c, target],
                   rsz_recv.at[c, source], where),
            remote(mean_z_send.at[c], mean_z.at[c, source], rmz_send.at[c, target],
                   rmz_recv.at[c, source], where),
        )

    def agz(c, target, source):
        rows_of = slab.at[c, pl.ds(pl.multiple_of(source * slim, slim), slim)]
        return remote(rows_of, rows_of, agz_send.at[c, target], agz_recv.at[c, source],
                      to_z(target))

    def agx(c, target, source):
        return remote(slab.at[c], full.at[c, source], agx_send.at[c, target],
                      agx_recv.at[c, source], to_x(target))

    def agm(target, source):
        return remote(mean_part.at[source], mean_part.at[source], agm_send.at[target],
                      agm_recv.at[source], to_x(target))

    def store(c, source, held):
        cols = pl.ds(pl.multiple_of(c * part + source * wide, wide), wide)
        return pltpu.make_async_copy(held, out_cov.at[:, cols], store_sem.at[c, source])

    def start_both(pair):
        pair[0].start()
        pair[1].start()

    def recv_both(pair):
        pair[0].wait_recv()
        pair[1].wait_recv()

    def gram_stage(c):
        others(sections, s, lambda k: smooth_copy(c, s, k).wait_recv())
        if c == 0:
            block = tokens[c, :, :, :BLOCK].reshape(shard_rows, BLOCK) * valid
            block_sum = lax.dot_general(block, valid, CONTRACT_ROWS, preferred_element_type=F32)
            kept["block"] = block
            kept["sum"] = block_sum[:, :1]
        for k in range(nx):
            here = tokens[c, :, :, k * wide:(k + 1) * wide].reshape(shard_rows, wide)
            mean_here = jnp.dot(valid_row, here, preferred_element_type=F32)[:1] * share
            if c == 0 and k == 0:
                kept["mean"] = mean_here[:, :BLOCK]
            moments = lax.dot_general(
                kept["block"], here, CONTRACT_ROWS, preferred_element_type=F32
            )
            gram[c, k] = (moments - kept["sum"] * mean_here).astype(BF16)
            mean_send[c, k, :, :wide] = mean_here
            mean_send[c, k, :, wide:wide + BLOCK] = kept["mean"]
            mean_send[c, k, :, wide + BLOCK:] = used
        others(nx, x, lambda k: start_both(rsx(c, k, x)))
        mean_x[c, x] = mean_send[c, x]

    def x_stage(c):
        others(nx, x, lambda k: recv_both(rsx(c, x, k)))
        joined, middle = merge_means(mean_x.at[c], nx, wide, spread.at[0])
        mean_z_send[c, :, :wide + BLOCK] = middle
        mean_z_send[c, :, wide + BLOCK:] = jnp.broadcast_to(joined, (1, BLOCK))

        def join(k, _):
            here = pl.ds(pl.multiple_of(k * slim, slim), slim)
            total = spread[0, here, :] + gram[c, x, here, :].astype(F32)
            for j in range(1, nx):
                total = total + gram_x[c, lax.rem(x + j, nx), here, :].astype(F32)
            part_z[c, k] = total.astype(BF16)
            return 0

        lax.fori_loop(0, nz, join, 0)
        others(nz, z, lambda k: start_both(rsz(c, k, z)))
        mean_z[c, z] = mean_z_send[c]
        gram_z[c, z] = part_z[c, z]

    def z_stage(c):
        others(nz, z, lambda k: recv_both(rsz(c, z, k)))
        joined, middle = merge_means(mean_z.at[c], nz, wide, spread.at[1])
        here = pl.ds(pl.multiple_of(z * slim, slim), slim)
        total = spread[1, here, :]
        for k in range(nz):
            total = total + gram_z[c, k].astype(F32)
        slab[c, here, :] = (total / joined).astype(BF16)
        mean_part[x, :, c * wide:(c + 1) * wide] = middle[:, :wide]
        others(nz, z, lambda k: agz(c, k, z).start())
        if c == CHUNKS - 1:
            others(nx, x, lambda k: agm(k, x).start())

    def a_stage(c):
        others(nz, z, lambda k: agz(c, z, k).wait_recv())
        others(nx, x, lambda k: agx(c, k, x).start())
        store(c, x, slab.at[c]).start()

    def b_stage(c):
        def arrived(k):
            agx(c, x, k).wait_recv()
            store(c, k, full.at[c, k]).start()

        others(nx, x, arrived)

    stages = (gram_stage, x_stage, z_stage, a_stage, b_stage)
    for tick in range(CHUNKS + len(stages) - 1):
        for place, stage in enumerate(stages):
            if 0 <= tick - place < CHUNKS:
                stage(tick - place)

    others(nx, x, lambda k: agm(x, k).wait_recv())
    for k in range(nx):
        for c in range(CHUNKS):
            place = c * part + k * wide
            mean_full[:, place:place + wide] = mean_part[k, :, c * wide:(c + 1) * wide]
    mean_store = pltpu.make_async_copy(mean_full, out_mean, mean_sem.at[0])
    mean_store.start()

    others(ny, y, lambda k: params_across(k).wait_send())
    params_over().wait_send()
    others(ny, y, lambda k: params_on(2 * k + core).wait_send())
    others(nx, x, lambda k: agm(k, x).wait_send())

    def finish(c, _):
        def end_x(k):
            rsx(c, k, x)[0].wait_send()
            rsx(c, k, x)[1].wait_send()
            agx(c, k, x).wait_send()
            store(c, k, full.at[c, k]).wait()

        def end_z(k):
            rsz(c, k, z)[0].wait_send()
            rsz(c, k, z)[1].wait_send()
            agz(c, k, z).wait_send()

        others(sections, s, lambda k: smooth_copy(c, k, s).wait_send())
        others(nx, x, end_x)
        others(nz, z, end_z)
        store(c, x, slab.at[c]).wait()
        return 0

    lax.fori_loop(0, CHUNKS, finish, 0)
    mean_store.wait()


def body(
    patches, patch_ids, pos_table, token_counts, norm_gain, norm_bias, branch_scale, act_range,
    weight_range, alpha_index,
):
    sections = lax.axis_size("section")
    toks = lax.axis_size("tok")
    nx, nz = RING_X, toks // RING_X
    width = patches.shape[1]
    rows = patches.shape[0] // sections
    part = width // CHUNKS
    wide = part // nx
    slim = BLOCK // nz
    meta = wide + 2 * BLOCK
    dma = pltpu.SemaphoreType.DMA
    smem = pl.BlockSpec(memory_space=pltpu.SMEM)
    hbm = pl.BlockSpec(memory_space=pl.ANY)
    vmem = pltpu.VMEM
    by_x, by_z = dma((CHUNKS, nx)), dma((CHUNKS, nz))
    by_section = dma((CHUNKS, sections))
    cov, mean = pl.pallas_call(
        functools.partial(kernel, sections, toks),
        out_shape=(
            jax.ShapeDtypeStruct((BLOCK, width), BF16),
            jax.ShapeDtypeStruct((1, width), F32),
        ),
        in_specs=[smem] * 3 + [hbm] * 7,
        out_specs=(hbm, hbm),
        scratch_shapes=[
            vmem((rows, width), BF16),
            vmem(pos_table.shape, BF16),
            vmem((2, 1, width), F32),
            vmem((sections, 4, 1, width), F32),
            vmem((rows, width), F32),
            vmem((CHUNKS, sections, rows, part), BF16),
            vmem((CHUNKS, sections, rows, part), BF16),
            vmem((CHUNKS, nx, BLOCK, wide), BF16),
            vmem((CHUNKS, nx, 1, meta), F32),
            vmem((CHUNKS, nx, BLOCK, wide), BF16),
            vmem((CHUNKS, nx, 1, meta), F32),
            vmem((CHUNKS, nz, slim, wide), BF16),
            vmem((CHUNKS, 1, meta), F32),
            vmem((CHUNKS, nz, slim, wide), BF16),
            vmem((CHUNKS, nz, 1, meta), F32),
            vmem((2, BLOCK, wide), F32),
            vmem((CHUNKS, BLOCK, wide), BF16),
            vmem((CHUNKS, nx, BLOCK, wide), BF16),
            vmem((nx, 1, CHUNKS * wide), F32),
            vmem((1, width), F32),
            dma((7,)),
            dma((sections // 2,)),
            dma((sections // 2,)),
            dma((sections,)),
            by_section,
            by_section,
            by_x, by_x, by_x, by_x,
            by_z, by_z, by_z, by_z,
            by_z, by_z,
            by_x, by_x,
            dma((nx,)),
            dma((nx,)),
            by_x,
            dma((1,)),
        ],
        compiler_params=pltpu.CompilerParams(
            collective_id=0, has_side_effects=True, vmem_limit_bytes=60 * 1024 * 1024
        ),
        name="moments",
    )(
        patch_ids, token_counts, alpha_index, patches, pos_table, norm_gain, norm_bias,
        branch_scale, act_range, weight_range,
    )
    return cov[None].astype(F32), mean


def solution(mesh):
    in_specs = (
        P("tok", None),
        P("tok"),
        P(),
        P("tok"),
        P("section", None),
        P("section", None),
        P("section", None),
        P("section", None),
        P("section", None),
        P("section"),
    )
    out_specs = (P("section", None, None), P("section", None))
    return jax.shard_map(body, mesh=mesh, in_specs=in_specs, out_specs=out_specs, check_vma=False)
```

```python
import functools

import jax
import jax.numpy as jnp
from jax import lax
from jax.experimental import pallas as pl
from jax.experimental.pallas import tpu as pltpu
from jax.sharding import PartitionSpec as P

BLOCK = 128
RING_X = 4
STEP = 768
CHUNKS = 4
EARLY = 0
F32 = jnp.float32
BF16 = jnp.bfloat16
MESH = pl.DeviceIdType.MESH
CONTRACT_ROWS = (((0,), (0,)), ((), ()))


def columns(c, size=STEP):
    return pl.ds(pl.multiple_of(c * size, size), size)


def fold_lanes(values):
    total = values[:, :128]
    for k in range(1, values.shape[1] // 128):
        total = total + values[:, k * 128:(k + 1) * 128]
    return total


def others(size, me, fn):
    def go(k, _):
        fn(lax.rem(me + k, size))
        return 0

    lax.fori_loop(1, size, go, 0)


def merge_means(means, size, wide, spread):
    rows_of = [means[k] for k in range(size)]
    counts = [one[:, wide + BLOCK:wide + BLOCK + 1] for one in rows_of]
    joined = functools.reduce(jnp.add, counts)
    middle = functools.reduce(
        jnp.add, [one[:, :wide + BLOCK] * n for one, n in zip(rows_of, counts)]
    ) / joined
    index = lax.broadcasted_iota(jnp.int32, (8, wide + BLOCK), 0)
    away = jnp.zeros((8, wide + BLOCK), F32)
    weight_of = jnp.zeros((8, 1), F32)
    index_one = lax.broadcasted_iota(jnp.int32, (8, 1), 0)
    for k in range(size):
        away = jnp.where(index == k, rows_of[k][:, :wide + BLOCK] - middle, away)
        weight_of = jnp.where(index_one == k, counts[k], weight_of)
    pushed = away[:, wide:] * weight_of
    spread[...] = lax.dot_general(
        pushed, away[:, :wide], CONTRACT_ROWS,
        precision=lax.Precision.HIGHEST, preferred_element_type=F32,
    )
    return joined, middle


def kernel(
    sections, toks, ids, count, alpha, patches, table, gain, bias, scale, act, weight, out_cov,
    out_mean, own_patches, table_here, ranges, params, hidden, smooth, tokens, counts, valid_row,
    block, block_sum, block_mean, part_z, mean_z_send, gram_z, mean_z, spread, slab, full,
    mean_part, mean_full, load_sem, par_send, par_pass, par_recv, cnt_send, cnt_recv, tok_send,
    tok_recv, rsz_send, rsz_recv, rmz_send, rmz_recv, agz_send, agz_recv, agx_send, agx_recv,
    agm_send, agm_recv, store_sem, mean_sem,
):
    s = lax.axis_index("section")
    t = lax.axis_index("tok")
    ny = sections // 2
    nx = RING_X
    nz = toks // nx
    y = lax.div(s, 2)
    core = lax.rem(s, 2)
    partner = s + 1 - 2 * core
    x = lax.rem(t, nx)
    z = lax.div(t, nx)
    width = patches.shape[1]
    rows = patches.shape[0] // sections
    part = width // CHUNKS
    wide = part // nx
    slim = BLOCK // nz
    steps = width // STEP

    def to_section(other):
        return {"section": other, "tok": t}

    def to_x(other):
        return {"section": s, "tok": z * nx + other}

    def to_z(other):
        return {"section": s, "tok": other * nx + x}

    def drain(held, sem):
        pltpu.make_async_copy(held, held, sem).wait()

    def remote(src, dst, send, recv, where):
        return pltpu.make_async_remote_copy(
            src_ref=src, dst_ref=dst, send_sem=send, recv_sem=recv, device_id=where,
            device_id_type=MESH,
        )

    loads = [
        pltpu.make_async_copy(act, ranges.at[0], load_sem.at[0]),
        pltpu.make_async_copy(weight, ranges.at[1], load_sem.at[1]),
        pltpu.make_async_copy(gain, params.at[s, 0], load_sem.at[2]),
        pltpu.make_async_copy(bias, params.at[s, 1], load_sem.at[3]),
        pltpu.make_async_copy(scale, params.at[s, 2], load_sem.at[4]),
        pltpu.make_async_copy(
            patches.at[pl.ds(pl.multiple_of(s * rows, rows), rows)], own_patches, load_sem.at[5]
        ),
        pltpu.make_async_copy(table, table_here, load_sem.at[6]),
    ]
    for load in loads:
        load.start()

    barrier = pltpu.get_barrier_semaphore()

    def greet(where):
        pl.semaphore_signal(barrier, inc=1, device_id=where, device_id_type=MESH)

    def greet_plane(k, _):
        to = lax.rem(x + lax.rem(k, nx), nx)
        greet({"section": lax.rem(s + lax.div(k, nx), sections), "tok": z * nx + to})
        return 0

    lax.fori_loop(1, sections * nx, greet_plane, 0)
    others(nz, z, lambda k: greet(to_z(k)))

    loads[0].wait()
    loads[1].wait()
    exponent = jnp.full((1, STEP), alpha[0], jnp.int32).astype(F32) / 8.0

    def factor_step(c, _):
        cols = columns(c)
        log_factor = exponent * jnp.log(ranges[0, :, cols]) + (exponent - 1.0) * jnp.log(
            ranges[1, :, cols]
        )
        params[s, 3, :, cols] = jnp.exp(-log_factor)
        return 0

    lax.fori_loop(0, steps, factor_step, 0)
    for load in loads[2:5]:
        load.wait()
    pl.semaphore_wait(barrier, sections * nx - 1 + nz - 1)

    def params_copy(layer, other, send):
        return remote(
            params.at[layer], params.at[layer], send, par_recv.at[layer], to_section(other)
        )

    def params_across(k):
        return params_copy(s, 2 * k + core, par_send.at[k])

    def params_over():
        return params_copy(s, partner, par_send.at[y])

    def params_on(layer):
        return params_copy(layer, partner, par_pass.at[lax.div(layer, 2)])

    others(ny, y, lambda k: params_across(k).start())
    params_over().start()
    counts[x] = jnp.full((1, 128), count[0], jnp.int32)

    def counts_copy(target, source):
        return remote(
            counts.at[source], counts.at[source], cnt_send.at[0], cnt_recv.at[0],
            to_x(target),
        )

    others(nx, x, lambda k: counts_copy(k, x).start())

    def pass_on(layer):
        @pl.when(jnp.logical_and(layer < sections, layer != s))
        def _():
            params_on(layer).wait_recv()
            params_on(layer).start()

    loads[5].wait()
    loads[6].wait()
    patch = lax.broadcasted_iota(jnp.int32, (rows, table.shape[0]), 1)
    row = lax.broadcasted_iota(jnp.int32, (rows, table.shape[0]), 0)
    wanted = jnp.zeros((rows, table.shape[0]), jnp.int32)
    for r in range(rows):
        wanted = jnp.where(row == r, ids[s * rows + r], wanted)
    pick = (patch == wanted).astype(F32).astype(BF16)

    def start_step(c, total):
        cols = columns(c)
        looked_up = jnp.dot(pick, table_here[:, cols], preferred_element_type=F32)
        first = (own_patches[:, cols].astype(F32) + looked_up).astype(BF16).astype(F32)
        hidden[:, cols] = first
        return total + fold_lanes(first)

    no_total = jnp.zeros((rows, 128), F32)
    first_total = lax.fori_loop(0, steps, start_step, no_total)
    pass_on(core)

    def part_cols(c):
        if c == 0:
            return pl.ds(0, BLOCK + wide)
        return pl.ds(BLOCK + c * wide, wide)

    def tok_copy(c, layer, to, source, at):
        cols = part_cols(c)
        return remote(
            smooth.at[layer * nx + to, :, cols], tokens.at[at * sections + source, :, cols],
            tok_send.at[c], tok_recv.at[c],
            {"section": layer, "tok": z * nx + to},
        )

    def send_layer(c, layer):
        def go(k, _):
            to = lax.rem(x + k, nx)

            @pl.when(jnp.logical_or(layer != s, to != x))
            def _():
                tok_copy(c, layer, to, s, x).start()

            return 0

        lax.fori_loop(0, nx, go, 0)

    def all_tok(fn):
        def go(k, _):
            fn(lax.rem(s + lax.div(k, nx), sections), lax.rem(x + lax.rem(k, nx), nx))
            return 0

        lax.fori_loop(1, sections * nx, go, 0)

    def layer_step(layer, total):
        mine = lax.rem(layer, 2) == core

        @pl.when(mine)
        def _():
            pass_on(layer + 2)

        @pl.when(jnp.logical_not(mine))
        def _():
            params_on(layer).wait_recv()

        centre = jnp.sum(total, axis=1, keepdims=True) * (1.0 / width)

        def spread_step(c, squares):
            away = hidden[:, columns(c)] - centre
            return squares + fold_lanes(away * away)

        squares = lax.fori_loop(0, steps, spread_step, no_total)
        variance = jnp.sum(squares, axis=1, keepdims=True) * (1.0 / width)
        inverse = lax.rsqrt(variance + 1e-06)
        new_total = no_total
        for c in range(CHUNKS):

            def value_step(k, so_far, c=c):
                cols = pl.ds(pl.multiple_of(c * part + k * STEP, STEP), STEP)
                current = hidden[:, cols]
                normed = (current - centre) * inverse * params[layer, 0, :, cols] + params[
                    layer, 1, :, cols
                ]
                smoothed = (normed * params[layer, 3, :, cols]).astype(BF16)
                for j in range(STEP // wide):
                    smooth[layer * nx + k * (STEP // wide) + j, :, BLOCK + c * wide:BLOCK + (c + 1) * wide] = (
                        smoothed[:, j * wide:(j + 1) * wide]
                    )
                inner = normed * (
                    0.7978845608028654 + 0.035677408136300125 * (normed * normed)
                )
                branch = 0.5 * normed * (1.0 + jnp.tanh(inner))
                updated = (current + params[layer, 2, :, cols] * branch).astype(BF16).astype(F32)
                hidden[:, cols] = updated
                return so_far + fold_lanes(updated)

            new_total = lax.fori_loop(0, part // STEP, value_step, new_total)
            if c == 0:
                for j in range(nx):
                    smooth[layer * nx + j, :, :BLOCK] = smooth[layer * nx, :, BLOCK:2 * BLOCK]
            if c < EARLY:
                send_layer(c, layer)

        return new_total

    lax.fori_loop(0, sections, layer_step, first_total)
    for c in range(CHUNKS):
        if c >= EARLY:
            all_tok(lambda layer, to, c=c: tok_copy(c, layer, to, s, x).start())
    tokens[x * sections + s] = smooth[s * nx + x]
    drain(counts.at[:nx - 1], cnt_recv.at[0])

    group = nx * sections * rows

    def rsz(c, target, source):
        where = to_z(target)
        return (
            remote(part_z.at[c, target], gram_z.at[c, source], rsz_send.at[c], rsz_recv.at[c],
                   where),
            remote(mean_z_send.at[c], mean_z.at[c, source], rmz_send.at[c], rmz_recv.at[c],
                   where),
        )

    def agz(c, target, source):
        rows_of = slab.at[c, pl.ds(pl.multiple_of(source * slim, slim), slim)]
        return remote(rows_of, rows_of, agz_send.at[c], agz_recv.at[c],
                      to_z(target))

    def agx(c, target, source):
        return remote(slab.at[c], full.at[c, source], agx_send.at[c],
                      agx_recv.at[c], to_x(target))

    def agm(target, source):
        return remote(mean_part.at[source], mean_part.at[source], agm_send.at[0],
                      agm_recv.at[0], to_x(target))

    def store(c, source, held):
        cols = pl.ds(pl.multiple_of(c * part + source * wide, wide), wide)
        return pltpu.make_async_copy(held, out_cov.at[:, cols], store_sem.at[c])

    def start_both(pair):
        pair[0].start()
        pair[1].start()

    def gram_stage(c):
        drain(tokens.at[:nx * sections - 1, :, part_cols(c)], tok_recv.at[c])
        used = functools.reduce(jnp.add, [counts[k] for k in range(nx)]).astype(F32)
        if c == 0:
            place = lax.broadcasted_iota(jnp.int32, (sections * rows, BLOCK), 0)
            across = lax.broadcasted_iota(jnp.int32, (16, sections * rows), 1)
            valid = []
            for k in range(nx):
                here = counts[k][:, :1]
                valid.append((place < here).astype(F32).astype(BF16))
                valid_row[:, k * sections * rows:(k + 1) * sections * rows] = (
                    (across < here).astype(F32).astype(BF16)
                )
            valid = jnp.concatenate(valid, axis=0)
            block[...] = tokens[:, :, :BLOCK].reshape(group, BLOCK) * valid
            block_sum[...] = lax.dot_general(
                block[...], valid, CONTRACT_ROWS, preferred_element_type=F32
            )
        here = tokens[:, :, BLOCK + c * wide:BLOCK + (c + 1) * wide].reshape(group, wide)
        mean_here = jnp.dot(valid_row[...], here, preferred_element_type=F32)[:1] / used[:, :1]
        if c == 0:
            first = tokens[:, :, :BLOCK].reshape(group, BLOCK)
            block_mean[...] = (
                jnp.dot(valid_row[...], first, preferred_element_type=F32)[:1] / used
            )
        moments = lax.dot_general(block[...], here, CONTRACT_ROWS, preferred_element_type=F32)
        moments = moments - block_sum[:, :1] * mean_here
        part_z[c] = moments.astype(BF16).reshape(nz, slim, wide)
        mean_z_send[c, :, :wide] = mean_here
        mean_z_send[c, :, wide:wide + BLOCK] = block_mean[...]
        mean_z_send[c, :, wide + BLOCK:] = used
        others(nz, z, lambda k: start_both(rsz(c, k, z)))
        mean_z[c, z] = mean_z_send[c]
        gram_z[c, z] = part_z[c, z]

    def z_stage(c):
        drain(mean_z.at[c, :nz - 1], rmz_recv.at[c])
        drain(gram_z.at[c, :nz - 1], rsz_recv.at[c])
        joined, middle = merge_means(mean_z.at[c], nz, wide, spread)
        here = pl.ds(pl.multiple_of(z * slim, slim), slim)
        total = spread[here, :]
        for k in range(nz):
            total = total + gram_z[c, k].astype(F32)
        slab[c, here, :] = (total / joined).astype(BF16)
        mean_part[x, :, c * wide:(c + 1) * wide] = middle[:, :wide]
        others(nz, z, lambda k: agz(c, k, z).start())
        if c == CHUNKS - 1:
            others(nx, x, lambda k: agm(k, x).start())

    def a_stage(c):
        drain(slab.at[c, :BLOCK - slim], agz_recv.at[c])
        others(nx, x, lambda k: agx(c, k, x).start())
        store(c, x, slab.at[c]).start()

    def b_stage(c):
        drain(full.at[c, :nx - 1], agx_recv.at[c])
        others(nx, x, lambda k: store(c, k, full.at[c, k]).start())

    stages = (gram_stage, z_stage, a_stage, b_stage)
    for tick in range(CHUNKS + len(stages) - 1):
        for place, stage in enumerate(stages):
            if 0 <= tick - place < CHUNKS:
                stage(tick - place)

    drain(mean_part.at[:nx - 1], agm_recv.at[0])
    for k in range(nx):
        for c in range(CHUNKS):
            place = c * part + k * wide
            mean_full[:, place:place + wide] = mean_part[k, :, c * wide:(c + 1) * wide]
    mean_store = pltpu.make_async_copy(mean_full, out_mean, mean_sem.at[0])
    mean_store.start()

    others(ny, y, lambda k: params_across(k).wait_send())
    params_over().wait_send()
    others(ny, y, lambda k: params_on(2 * k + core).wait_send())
    drain(mean_part.at[:nx - 1], agm_send.at[0])

    drain(counts.at[:nx - 1], cnt_send.at[0])

    for c in range(CHUNKS):
        drain(smooth.at[:nx * sections - 1, :, part_cols(c)], tok_send.at[c])
        drain(part_z.at[c, :nz - 1], rsz_send.at[c])
        drain(mean_z.at[c, :nz - 1], rmz_send.at[c])
        drain(slab.at[c, :BLOCK - slim], agz_send.at[c])
        drain(full.at[c, :nx - 1], agx_send.at[c])
        drain(out_cov.at[:, c * part:(c + 1) * part], store_sem.at[c])
    mean_store.wait()


def body(
    patches, patch_ids, pos_table, token_counts, norm_gain, norm_bias, branch_scale, act_range,
    weight_range, alpha_index,
):
    sections = lax.axis_size("section")
    toks = lax.axis_size("tok")
    nx, nz = RING_X, toks // RING_X
    width = patches.shape[1]
    rows = patches.shape[0] // sections
    part = width // CHUNKS
    wide = part // nx
    slim = BLOCK // nz
    meta = wide + 2 * BLOCK
    dma = pltpu.SemaphoreType.DMA
    smem = pl.BlockSpec(memory_space=pltpu.SMEM)
    hbm = pl.BlockSpec(memory_space=pl.ANY)
    vmem = pltpu.VMEM
    each = dma((CHUNKS,))
    group = nx * sections * rows
    cov, mean = pl.pallas_call(
        functools.partial(kernel, sections, toks),
        out_shape=(
            jax.ShapeDtypeStruct((BLOCK, width), BF16),
            jax.ShapeDtypeStruct((1, width), F32),
        ),
        in_specs=[smem] * 3 + [hbm] * 7,
        out_specs=(hbm, hbm),
        scratch_shapes=[
            vmem((rows, width), BF16),
            vmem(pos_table.shape, BF16),
            vmem((2, 1, width), F32),
            vmem((sections, 4, 1, width), F32),
            vmem((rows, width), F32),
            vmem((sections * nx, rows, BLOCK + CHUNKS * wide), BF16),
            vmem((nx * sections, rows, BLOCK + CHUNKS * wide), BF16),
            vmem((nx, 1, 128), jnp.int32),
            vmem((16, group), BF16),
            vmem((group, BLOCK), BF16),
            vmem((BLOCK, BLOCK), F32),
            vmem((1, BLOCK), F32),
            vmem((CHUNKS, nz, slim, wide), BF16),
            vmem((CHUNKS, 1, meta), F32),
            vmem((CHUNKS, nz, slim, wide), BF16),
            vmem((CHUNKS, nz, 1, meta), F32),
            vmem((BLOCK, wide), F32),
            vmem((CHUNKS, BLOCK, wide), BF16),
            vmem((CHUNKS, nx, BLOCK, wide), BF16),
            vmem((nx, 1, CHUNKS * wide), F32),
            vmem((1, width), F32),
            dma((7,)),
            dma((sections // 2,)),
            dma((sections // 2,)),
            dma((sections,)),
            dma((1,)),
            dma((1,)),
            each, each,
            each, each, each, each,
            each, each,
            each, each,
            dma((1,)),
            dma((1,)),
            each,
            dma((1,)),
        ],
        compiler_params=pltpu.CompilerParams(
            collective_id=0, has_side_effects=True, vmem_limit_bytes=60 * 1024 * 1024
        ),
        name="moments",
    )(
        patch_ids, token_counts, alpha_index, patches, pos_table, norm_gain, norm_bias,
        branch_scale, act_range, weight_range,
    )
    return cov[None].astype(F32), mean


def solution(mesh):
    in_specs = (
        P("tok", None),
        P("tok"),
        P(),
        P("tok"),
        P("section", None),
        P("section", None),
        P("section", None),
        P("section", None),
        P("section", None),
        P("section"),
    )
    out_specs = (P("section", None, None), P("section", None))
    return jax.shard_map(body, mesh=mesh, in_specs=in_specs, out_specs=out_specs, check_vma=False)
```

```python
import functools

import jax
import jax.numpy as jnp
from jax import lax
from jax.experimental import pallas as pl
from jax.experimental.pallas import tpu as pltpu
from jax.sharding import PartitionSpec as P

BLOCK = 128
RING_X = 4
STEP = 768
UNITS = (3, 3, 3, 3)
SWAPPED = ()
WIDES = [128 * n for n in UNITS]
STARTS = [sum(WIDES[:k]) for k in range(len(WIDES))]
CHUNKS = len(WIDES)
F32 = jnp.float32
BF16 = jnp.bfloat16
MESH = pl.DeviceIdType.MESH
CONTRACT_ROWS = (((0,), (0,)), ((), ()))


def columns(c, size=STEP):
    return pl.ds(pl.multiple_of(c * size, size), size)


def fold_lanes(values):
    total = values[:, :128]
    for k in range(1, values.shape[1] // 128):
        total = total + values[:, k * 128:(k + 1) * 128]
    return total


def others(size, me, fn):
    def go(k, _):
        fn(lax.rem(me + k, size))
        return 0

    lax.fori_loop(1, size, go, 0)


def merge_means(means, size, wide, spread):
    rows_of = [means[k] for k in range(size)]
    counts = [one[:, BLOCK:BLOCK + 1] for one in rows_of]
    joined = functools.reduce(jnp.add, counts)

    def apart(start, extent):
        pieces = [one[:, start:start + extent] for one in rows_of]
        middle = functools.reduce(jnp.add, [one * n for one, n in zip(pieces, counts)]) / joined
        index = lax.broadcasted_iota(jnp.int32, (8, extent), 0)
        away = jnp.zeros((8, extent), F32)
        for k in range(size):
            away = jnp.where(index == k, pieces[k] - middle, away)
        return away, middle

    index_one = lax.broadcasted_iota(jnp.int32, (8, 1), 0)
    weight_of = jnp.zeros((8, 1), F32)
    for k in range(size):
        weight_of = jnp.where(index_one == k, counts[k], weight_of)
    pushed, _ = apart(0, BLOCK)
    away, middle = apart(2 * BLOCK, wide)
    spread[:, :wide] = lax.dot_general(
        pushed * weight_of, away, CONTRACT_ROWS,
        precision=lax.Precision.HIGHEST, preferred_element_type=F32,
    )
    return joined, middle


def kernel(
    sections, toks, ids, count, alpha, patches, table, gain, bias, scale, act, weight, final,
    mean_full, own_patches, table_here, ranges, params, hidden, smooth, tokens, counts, valid_row,
    block, block_sum, block_mean, part_z, mean_z_send, gram_z, mean_z, spread, mean_part,
    load_sem, par_send, par_pass, par_recv, cnt_send, cnt_recv, tok_send,
    tok_recv, rsz_send, rsz_recv, rmz_send, rmz_recv, agz_send, agz_recv, agx_send, agx_recv,
    agm_send, agm_recv,
):
    s = lax.axis_index("section")
    t = lax.axis_index("tok")
    ny = sections // 2
    nx = RING_X
    nz = toks // nx
    y = lax.div(s, 2)
    core = lax.rem(s, 2)
    partner = s + 1 - 2 * core
    x = lax.rem(t, nx)
    z = lax.div(t, nx)
    width = patches.shape[1]
    rows = patches.shape[0] // sections
    slim = BLOCK // nz
    steps = width // STEP

    def to_section(other):
        return {"section": other, "tok": t}

    def to_x(other):
        return {"section": s, "tok": z * nx + other}

    def to_z(other):
        return {"section": s, "tok": other * nx + x}

    def drain(held, sem):
        pltpu.make_async_copy(held, held, sem).wait()

    def remote(src, dst, send, recv, where):
        return pltpu.make_async_remote_copy(
            src_ref=src, dst_ref=dst, send_sem=send, recv_sem=recv, device_id=where,
            device_id_type=MESH,
        )

    loads = [
        pltpu.make_async_copy(act, ranges.at[0], load_sem.at[0]),
        pltpu.make_async_copy(weight, ranges.at[1], load_sem.at[1]),
        pltpu.make_async_copy(gain, params.at[s, 0], load_sem.at[2]),
        pltpu.make_async_copy(bias, params.at[s, 1], load_sem.at[3]),
        pltpu.make_async_copy(scale, params.at[s, 2], load_sem.at[4]),
        pltpu.make_async_copy(
            patches.at[pl.ds(pl.multiple_of(s * rows, rows), rows)], own_patches, load_sem.at[5]
        ),
        pltpu.make_async_copy(table, table_here, load_sem.at[6]),
    ]
    for load in loads:
        load.start()

    barrier = pltpu.get_barrier_semaphore()

    def greet(where):
        pl.semaphore_signal(barrier, inc=1, device_id=where, device_id_type=MESH)

    def greet_plane(k, _):
        to = lax.rem(x + lax.rem(k, nx), nx)
        greet({"section": lax.rem(s + lax.div(k, nx), sections), "tok": z * nx + to})
        return 0

    lax.fori_loop(1, sections * nx, greet_plane, 0)
    others(nz, z, lambda k: greet(to_z(k)))

    loads[0].wait()
    loads[1].wait()
    exponent = jnp.full((1, STEP), alpha[0], jnp.int32).astype(F32) / 8.0

    def factor_step(c, _):
        cols = columns(c)
        log_factor = exponent * jnp.log(ranges[0, :, cols]) + (exponent - 1.0) * jnp.log(
            ranges[1, :, cols]
        )
        params[s, 3, :, cols] = jnp.exp(-log_factor)
        return 0

    lax.fori_loop(0, steps, factor_step, 0)
    for load in loads[2:5]:
        load.wait()
    pl.semaphore_wait(barrier, sections * nx - 1 + nz - 1)

    def params_copy(layer, other, send):
        return remote(
            params.at[layer], params.at[layer], send, par_recv.at[layer], to_section(other)
        )

    def params_across(k):
        return params_copy(s, 2 * k + core, par_send.at[k])

    def params_over():
        return params_copy(s, partner, par_send.at[y])

    def params_on(layer):
        return params_copy(layer, partner, par_pass.at[lax.div(layer, 2)])

    others(ny, y, lambda k: params_across(k).start())
    params_over().start()
    counts[x] = jnp.full((1, 128), count[0], jnp.int32)

    def counts_copy(target, source):
        return remote(
            counts.at[source], counts.at[source], cnt_send.at[0], cnt_recv.at[0],
            to_x(target),
        )

    others(nx, x, lambda k: counts_copy(k, x).start())

    def pass_on(layer):
        @pl.when(jnp.logical_and(layer < sections, layer != s))
        def _():
            params_on(layer).wait_recv()
            params_on(layer).start()

    loads[5].wait()
    loads[6].wait()
    patch = lax.broadcasted_iota(jnp.int32, (rows, table.shape[0]), 1)
    row = lax.broadcasted_iota(jnp.int32, (rows, table.shape[0]), 0)
    wanted = jnp.zeros((rows, table.shape[0]), jnp.int32)
    for r in range(rows):
        wanted = jnp.where(row == r, ids[s * rows + r], wanted)
    pick = (patch == wanted).astype(F32).astype(BF16)

    def start_step(c, total):
        cols = columns(c)
        looked_up = jnp.dot(pick, table_here[:, cols], preferred_element_type=F32)
        first = (own_patches[:, cols].astype(F32) + looked_up).astype(BF16).astype(F32)
        hidden[:, cols] = first
        return total + fold_lanes(first)

    no_total = jnp.zeros((rows, 128), F32)
    first_total = lax.fori_loop(0, steps, start_step, no_total)
    pass_on(core)

    def part_cols(c):
        if c == 0:
            return pl.ds(0, BLOCK + WIDES[0])
        return pl.ds(BLOCK + STARTS[c], WIDES[c])

    def quarter_cols(c):
        return pl.ds(STARTS[c], WIDES[c])

    def own_cols(c, of):
        return pl.ds(pl.multiple_of(nx * STARTS[c] + of * WIDES[c], BLOCK), WIDES[c])

    def all_cols(c):
        return pl.ds(nx * STARTS[c], nx * WIDES[c])

    def tok_copy(c, layer, to, source, at):
        cols = part_cols(c)
        return remote(
            smooth.at[layer * nx + to, :, cols], tokens.at[at * sections + source, :, cols],
            tok_send.at[c], tok_recv.at[c],
            {"section": layer, "tok": z * nx + to},
        )

    def all_tok(fn):
        def go(k, _):
            fn(lax.rem(s + lax.rem(k, sections), sections), lax.rem(x + lax.div(k, sections), nx))
            return 0

        lax.fori_loop(1, sections * nx, go, 0)

    def layer_step(layer, total):
        mine = lax.rem(layer, 2) == core

        @pl.when(mine)
        def _():
            pass_on(layer + 2)

        @pl.when(jnp.logical_not(mine))
        def _():
            params_on(layer).wait_recv()

        centre = jnp.sum(total, axis=1, keepdims=True) * (1.0 / width)

        def spread_step(c, squares):
            away = hidden[:, columns(c)] - centre
            return squares + fold_lanes(away * away)

        squares = lax.fori_loop(0, steps, spread_step, no_total)
        variance = jnp.sum(squares, axis=1, keepdims=True) * (1.0 / width)
        inverse = lax.rsqrt(variance + 1e-06)
        new_total = no_total
        for c in range(CHUNKS):
            for j in range(nx):
                start = nx * STARTS[c] + j * WIDES[c]
                cols = slice(start, start + WIDES[c])
                current = hidden[:, cols]
                normed = (current - centre) * inverse * params[layer, 0, :, cols] + params[
                    layer, 1, :, cols
                ]
                smoothed = (normed * params[layer, 3, :, cols]).astype(BF16)
                place = BLOCK + STARTS[c]
                smooth[layer * nx + j, :, place:place + WIDES[c]] = smoothed
                if c == 0 and j == 0:
                    for k in range(nx):
                        smooth[layer * nx + k, :, :BLOCK] = smoothed[:, :BLOCK]
                inner = normed * (
                    0.7978845608028654 + 0.035677408136300125 * (normed * normed)
                )
                branch = 0.5 * normed * (1.0 + jnp.tanh(inner))
                updated = (current + params[layer, 2, :, cols] * branch).astype(BF16).astype(F32)
                hidden[:, cols] = updated
                new_total = new_total + fold_lanes(updated)
        return new_total

    lax.fori_loop(0, sections, layer_step, first_total)
    for c in range(CHUNKS):
        all_tok(lambda layer, to, c=c: tok_copy(c, layer, to, s, x).start())
    tokens[x * sections + s] = smooth[s * nx + x]
    drain(counts.at[:nx - 1], cnt_recv.at[0])

    group = nx * sections * rows

    def rsz(c, target, source):
        where = to_z(target)
        cols = quarter_cols(c)
        meta = pl.ds(0, 2 * BLOCK + WIDES[c])
        return (
            remote(part_z.at[target, :, cols], gram_z.at[source, :, cols], rsz_send.at[c],
                   rsz_recv.at[c], where),
            remote(mean_z_send.at[c, :, meta], mean_z.at[c, source, :, meta], rmz_send.at[c],
                   rmz_recv.at[c], where),
        )

    def along_z(c, target):
        cols = all_cols(c) if c in SWAPPED else own_cols(c, x)
        held = final.at[z, :, cols]
        return remote(held, held, agz_send.at[c], agz_recv.at[c], to_z(target))

    def along_x(c, target):
        cols = own_cols(c, x)
        held = final.at[z, :, cols] if c in SWAPPED else final.at[:, :, cols]
        return remote(held, held, agx_send.at[c], agx_recv.at[c], to_x(target))

    def drain_z(c, sem):
        size = nx * WIDES[c] if c in SWAPPED else WIDES[c]
        drain(final.at[:nz - 1, :, :size], sem.at[c])

    def drain_x(c, sem):
        size = (nx - 1) * WIDES[c]
        drain(final.at[0, :, :size] if c in SWAPPED else final.at[:, :, :size], sem.at[c])

    def agm(target, source):
        return remote(mean_part.at[source], mean_part.at[source], agm_send.at[0],
                      agm_recv.at[0], to_x(target))

    def start_both(pair):
        pair[0].start()
        pair[1].start()

    def gram_stage(c):
        drain(tokens.at[:nx * sections - 1, :, part_cols(c)], tok_recv.at[c])
        used = functools.reduce(jnp.add, [counts[k] for k in range(nx)]).astype(F32)
        if c == 0:
            place = lax.broadcasted_iota(jnp.int32, (sections * rows, BLOCK), 0)
            across = lax.broadcasted_iota(jnp.int32, (16, sections * rows), 1)
            valid = []
            for k in range(nx):
                here = counts[k][:, :1]
                valid.append((place < here).astype(F32).astype(BF16))
                valid_row[:, k * sections * rows:(k + 1) * sections * rows] = (
                    (across < here).astype(F32).astype(BF16)
                )
            valid = jnp.concatenate(valid, axis=0)
            block[...] = tokens[:, :, :BLOCK].reshape(group, BLOCK) * valid
            block_sum[...] = lax.dot_general(
                block[...], valid, CONTRACT_ROWS, preferred_element_type=F32
            )
        wide, start = WIDES[c], STARTS[c]
        here = tokens[:, :, BLOCK + start:BLOCK + start + wide].reshape(group, wide)
        mean_here = jnp.dot(valid_row[...], here, preferred_element_type=F32)[:1] / used[:, :1]
        if c == 0:
            first = tokens[:, :, :BLOCK].reshape(group, BLOCK)
            block_mean[...] = (
                jnp.dot(valid_row[...], first, preferred_element_type=F32)[:1] / used
            )
        moments = lax.dot_general(block[...], here, CONTRACT_ROWS, preferred_element_type=F32)
        moments = moments - block_sum[:, :1] * mean_here
        part_z[:, :, start:start + wide] = moments.astype(BF16).reshape(nz, slim, wide)
        mean_z_send[c, :, :BLOCK] = block_mean[...]
        mean_z_send[c, :, BLOCK:2 * BLOCK] = used
        mean_z_send[c, :, 2 * BLOCK:2 * BLOCK + wide] = mean_here
        others(nz, z, lambda k: start_both(rsz(c, k, z)))
        mean_z[c, z] = mean_z_send[c]
        gram_z[z, :, start:start + wide] = part_z[z, :, start:start + wide]

    def z_stage(c):
        wide, start = WIDES[c], STARTS[c]
        drain(mean_z.at[c, :nz - 1, :, :2 * BLOCK + wide], rmz_recv.at[c])
        drain(gram_z.at[:nz - 1, :, :wide], rsz_recv.at[c])
        joined, middle = merge_means(mean_z.at[c], nz, wide, spread)
        total = spread[pl.ds(pl.multiple_of(z * slim, slim), slim), :wide]
        for k in range(nz):
            total = total + gram_z[k, :, start:start + wide].astype(F32)
        final[z, :, own_cols(c, x)] = (total / joined).astype(BF16)
        mean_part[x, :, start:start + wide] = middle
        if c in SWAPPED:
            others(nx, x, lambda k: along_x(c, k).start())
        else:
            others(nz, z, lambda k: along_z(c, k).start())
        if c == CHUNKS - 1:
            others(nx, x, lambda k: agm(k, x).start())

    def a_stage(c):
        if c in SWAPPED:
            drain_x(c, agx_recv)
            others(nz, z, lambda k: along_z(c, k).start())
        else:
            drain_z(c, agz_recv)
            others(nx, x, lambda k: along_x(c, k).start())

    def b_stage(c):
        if c in SWAPPED:
            drain_z(c, agz_recv)
        else:
            drain_x(c, agx_recv)

    stages = (gram_stage, z_stage, a_stage, b_stage)
    for tick in range(CHUNKS + len(stages) - 1):
        for place, stage in enumerate(stages):
            if 0 <= tick - place < CHUNKS:
                stage(tick - place)

    drain(mean_part.at[:nx - 1], agm_recv.at[0])
    for k in range(nx):
        for c in range(CHUNKS):
            start, wide = STARTS[c], WIDES[c]
            place = nx * start + k * wide
            mean_full[:, place:place + wide] = mean_part[k, :, start:start + wide]

    others(ny, y, lambda k: params_across(k).wait_send())
    params_over().wait_send()
    others(ny, y, lambda k: params_on(2 * k + core).wait_send())
    drain(mean_part.at[:nx - 1], agm_send.at[0])

    drain(counts.at[:nx - 1], cnt_send.at[0])

    for c in range(CHUNKS):
        drain(smooth.at[:nx * sections - 1, :, part_cols(c)], tok_send.at[c])
        drain(part_z.at[:nz - 1, :, :WIDES[c]], rsz_send.at[c])
        drain(mean_z.at[c, :nz - 1, :, :2 * BLOCK + WIDES[c]], rmz_send.at[c])
        drain_z(c, agz_send)
        drain_x(c, agx_send)


def body(
    patches, patch_ids, pos_table, token_counts, norm_gain, norm_bias, branch_scale, act_range,
    weight_range, alpha_index,
):
    sections = lax.axis_size("section")
    toks = lax.axis_size("tok")
    nx, nz = RING_X, toks // RING_X
    width = patches.shape[1]
    rows = patches.shape[0] // sections
    quarter = width // nx
    slim = BLOCK // nz
    widest = max(WIDES)
    meta = widest + 2 * BLOCK
    dma = pltpu.SemaphoreType.DMA
    smem = pl.BlockSpec(memory_space=pltpu.SMEM)
    hbm = pl.BlockSpec(memory_space=pltpu.HBM)
    on_chip = pl.BlockSpec(memory_space=pltpu.VMEM)
    vmem = pltpu.VMEM
    each = dma((CHUNKS,))
    group = nx * sections * rows
    cov, mean = pl.pallas_call(
        functools.partial(kernel, sections, toks),
        out_shape=(
            pltpu.VMEM((nz, slim, width), BF16),
            pltpu.VMEM((1, width), F32),
        ),
        in_specs=[smem] * 3 + [hbm] * 7,
        out_specs=(on_chip, on_chip),
        scratch_shapes=[
            vmem((rows, width), BF16),
            vmem(pos_table.shape, BF16),
            vmem((2, 1, width), F32),
            vmem((sections, 4, 1, width), F32),
            vmem((rows, width), F32),
            vmem((sections * nx, rows, BLOCK + quarter), BF16),
            vmem((nx * sections, rows, BLOCK + quarter), BF16),
            vmem((nx, 1, 128), jnp.int32),
            vmem((16, group), BF16),
            vmem((group, BLOCK), BF16),
            vmem((BLOCK, BLOCK), F32),
            vmem((1, BLOCK), F32),
            vmem((nz, slim, quarter), BF16),
            vmem((CHUNKS, 1, meta), F32),
            vmem((nz, slim, quarter), BF16),
            vmem((CHUNKS, nz, 1, meta), F32),
            vmem((BLOCK, widest), F32),
            vmem((nx, 1, quarter), F32),
            dma((7,)),
            dma((sections // 2,)),
            dma((sections // 2,)),
            dma((sections,)),
            dma((1,)),
            dma((1,)),
            each, each,
            each, each, each, each,
            each, each,
            each, each,
            dma((1,)),
            dma((1,)),
        ],
        compiler_params=pltpu.CompilerParams(
            collective_id=0, has_side_effects=True, vmem_limit_bytes=58 * 1024 * 1024
        ),
        name="moments",
    )(
        patch_ids, token_counts, alpha_index, patches, pos_table, norm_gain, norm_bias,
        branch_scale, act_range, weight_range,
    )
    return cov.reshape(1, BLOCK, width).astype(F32), mean


def solution(mesh):
    in_specs = (
        P("tok", None),
        P("tok"),
        P(),
        P("tok"),
        P("section", None),
        P("section", None),
        P("section", None),
        P("section", None),
        P("section", None),
        P("section"),
    )
    out_specs = (P("section", None, None), P("section", None))
    return jax.shard_map(body, mesh=mesh, in_specs=in_specs, out_specs=out_specs, check_vma=False)
```

```python
import functools

import jax
import jax.numpy as jnp
from jax import lax
from jax.experimental import pallas as pl
from jax.experimental.pallas import tpu as pltpu
from jax.sharding import PartitionSpec as P

BLOCK = 128
RING_X = 4
STEP = 768
UNITS = (3, 3, 3, 3)
SWAPPED = ()
RELAY = 3
WIDES = [128 * n for n in UNITS]
STARTS = [sum(WIDES[:k]) for k in range(len(WIDES))]
CHUNKS = len(WIDES)
F32 = jnp.float32
BF16 = jnp.bfloat16
MESH = pl.DeviceIdType.MESH
CONTRACT_ROWS = (((0,), (0,)), ((), ()))


def columns(c, size=STEP):
    return pl.ds(pl.multiple_of(c * size, size), size)


def fold_lanes(values):
    total = values[:, :128]
    for k in range(1, values.shape[1] // 128):
        total = total + values[:, k * 128:(k + 1) * 128]
    return total


def others(size, me, fn):
    def go(k, _):
        fn(lax.rem(me + k, size))
        return 0

    lax.fori_loop(1, size, go, 0)


def merge_means(means, size, wide, spread):
    rows_of = [means[k] for k in range(size)]
    counts = [one[:, BLOCK:BLOCK + 1] for one in rows_of]
    joined = functools.reduce(jnp.add, counts)

    def apart(start, extent):
        pieces = [one[:, start:start + extent] for one in rows_of]
        middle = functools.reduce(jnp.add, [one * n for one, n in zip(pieces, counts)]) / joined
        index = lax.broadcasted_iota(jnp.int32, (8, extent), 0)
        away = jnp.zeros((8, extent), F32)
        for k in range(size):
            away = jnp.where(index == k, pieces[k] - middle, away)
        return away, middle

    index_one = lax.broadcasted_iota(jnp.int32, (8, 1), 0)
    weight_of = jnp.zeros((8, 1), F32)
    for k in range(size):
        weight_of = jnp.where(index_one == k, counts[k], weight_of)
    pushed, _ = apart(0, BLOCK)
    away, middle = apart(2 * BLOCK, wide)
    spread[:, :wide] = lax.dot_general(
        pushed * weight_of, away, CONTRACT_ROWS,
        precision=lax.Precision.HIGHEST, preferred_element_type=F32,
    )
    return joined, middle


def kernel(
    sections, toks, ids, count, alpha, patches, table, gain, bias, scale, act, weight, final,
    mean_full, own_patches, table_here, ranges, params, hidden, smooth, tokens, counts, valid_row,
    block, block_sum, block_mean, part_z, mean_z_send, gram_z, mean_z, spread, mean_part,
    load_sem, par_send, par_pass, par_recv, cnt_send, cnt_recv, tok_send,
    tok_recv, rsz_send, rsz_recv, rmz_send, rmz_recv, agz_send, agz_recv, agx_send, agx_recv,
    near_send, near_recv, relay_send, relay_recv,
    agm_send, agm_recv,
):
    s = lax.axis_index("section")
    t = lax.axis_index("tok")
    ny = sections // 2
    nx = RING_X
    nz = toks // nx
    y = lax.div(s, 2)
    core = lax.rem(s, 2)
    partner = s + 1 - 2 * core
    x = lax.rem(t, nx)
    z = lax.div(t, nx)
    width = patches.shape[1]
    rows = patches.shape[0] // sections
    slim = BLOCK // nz
    steps = width // STEP

    def to_section(other):
        return {"section": other, "tok": t}

    def to_x(other):
        return {"section": s, "tok": z * nx + other}

    def to_z(other):
        return {"section": s, "tok": other * nx + x}

    def drain(held, sem):
        pltpu.make_async_copy(held, held, sem).wait()

    def remote(src, dst, send, recv, where):
        return pltpu.make_async_remote_copy(
            src_ref=src, dst_ref=dst, send_sem=send, recv_sem=recv, device_id=where,
            device_id_type=MESH,
        )

    loads = [
        pltpu.make_async_copy(act, ranges.at[0], load_sem.at[0]),
        pltpu.make_async_copy(weight, ranges.at[1], load_sem.at[1]),
        pltpu.make_async_copy(gain, params.at[s, 0], load_sem.at[2]),
        pltpu.make_async_copy(bias, params.at[s, 1], load_sem.at[3]),
        pltpu.make_async_copy(scale, params.at[s, 2], load_sem.at[4]),
        pltpu.make_async_copy(
            patches.at[pl.ds(pl.multiple_of(s * rows, rows), rows)], own_patches, load_sem.at[5]
        ),
        pltpu.make_async_copy(table, table_here, load_sem.at[6]),
    ]
    for load in loads:
        load.start()

    barrier = pltpu.get_barrier_semaphore()

    def greet(where):
        pl.semaphore_signal(barrier, inc=1, device_id=where, device_id_type=MESH)

    def greet_plane(k, _):
        to = lax.rem(x + lax.rem(k, nx), nx)
        greet({"section": lax.rem(s + lax.div(k, nx), sections), "tok": z * nx + to})
        return 0

    lax.fori_loop(1, sections * nx, greet_plane, 0)
    others(nz, z, lambda k: greet(to_z(k)))

    loads[0].wait()
    loads[1].wait()
    exponent = jnp.full((1, STEP), alpha[0], jnp.int32).astype(F32) / 8.0

    def factor_step(c, _):
        cols = columns(c)
        log_factor = exponent * jnp.log(ranges[0, :, cols]) + (exponent - 1.0) * jnp.log(
            ranges[1, :, cols]
        )
        params[s, 3, :, cols] = jnp.exp(-log_factor)
        return 0

    lax.fori_loop(0, steps, factor_step, 0)
    for load in loads[2:5]:
        load.wait()
    pl.semaphore_wait(barrier, sections * nx - 1 + nz - 1)

    def params_copy(layer, other, send):
        return remote(
            params.at[layer], params.at[layer], send, par_recv.at[layer], to_section(other)
        )

    def params_across(k):
        return params_copy(s, 2 * k + core, par_send.at[k])

    def params_over():
        return params_copy(s, partner, par_send.at[y])

    def params_on(layer):
        return params_copy(layer, partner, par_pass.at[lax.div(layer, 2)])

    others(ny, y, lambda k: params_across(k).start())
    params_over().start()
    counts[x] = jnp.full((1, 128), count[0], jnp.int32)

    def counts_copy(target, source):
        return remote(
            counts.at[source], counts.at[source], cnt_send.at[0], cnt_recv.at[0],
            to_x(target),
        )

    others(nx, x, lambda k: counts_copy(k, x).start())

    def pass_on(layer):
        @pl.when(jnp.logical_and(layer < sections, layer != s))
        def _():
            params_on(layer).wait_recv()
            params_on(layer).start()

    loads[5].wait()
    loads[6].wait()
    patch = lax.broadcasted_iota(jnp.int32, (rows, table.shape[0]), 1)
    row = lax.broadcasted_iota(jnp.int32, (rows, table.shape[0]), 0)
    wanted = jnp.zeros((rows, table.shape[0]), jnp.int32)
    for r in range(rows):
        wanted = jnp.where(row == r, ids[s * rows + r], wanted)
    pick = (patch == wanted).astype(F32).astype(BF16)

    def start_step(c, total):
        cols = columns(c)
        looked_up = jnp.dot(pick, table_here[:, cols], preferred_element_type=F32)
        first = (own_patches[:, cols].astype(F32) + looked_up).astype(BF16).astype(F32)
        hidden[:, cols] = first
        return total + fold_lanes(first)

    no_total = jnp.zeros((rows, 128), F32)
    first_total = lax.fori_loop(0, steps, start_step, no_total)
    pass_on(core)

    def part_cols(c):
        if c == 0:
            return pl.ds(0, BLOCK + WIDES[0])
        return pl.ds(BLOCK + STARTS[c], WIDES[c])

    def quarter_cols(c):
        return pl.ds(STARTS[c], WIDES[c])

    def own_cols(c, of):
        return pl.ds(pl.multiple_of(nx * STARTS[c] + of * WIDES[c], BLOCK), WIDES[c])

    def all_cols(c):
        return pl.ds(nx * STARTS[c], nx * WIDES[c])

    def tok_copy(c, layer, to, source, at):
        cols = part_cols(c)
        return remote(
            smooth.at[layer * nx + to, :, cols], tokens.at[at * sections + source, :, cols],
            tok_send.at[c], tok_recv.at[c],
            {"section": layer, "tok": z * nx + to},
        )

    def all_tok(fn):
        def go(k, _):
            fn(lax.rem(s + lax.rem(k, sections), sections), lax.rem(x + lax.div(k, sections), nx))
            return 0

        lax.fori_loop(1, sections * nx, go, 0)

    def layer_step(layer, total):
        mine = lax.rem(layer, 2) == core

        @pl.when(mine)
        def _():
            pass_on(layer + 2)

        @pl.when(jnp.logical_not(mine))
        def _():
            params_on(layer).wait_recv()

        centre = jnp.sum(total, axis=1, keepdims=True) * (1.0 / width)

        def spread_step(c, squares):
            away = hidden[:, columns(c)] - centre
            return squares + fold_lanes(away * away)

        squares = lax.fori_loop(0, steps, spread_step, no_total)
        variance = jnp.sum(squares, axis=1, keepdims=True) * (1.0 / width)
        inverse = lax.rsqrt(variance + 1e-06)
        new_total = no_total
        for c in range(CHUNKS):
            for j in range(nx):
                start = nx * STARTS[c] + j * WIDES[c]
                cols = slice(start, start + WIDES[c])
                current = hidden[:, cols]
                normed = (current - centre) * inverse * params[layer, 0, :, cols] + params[
                    layer, 1, :, cols
                ]
                smoothed = (normed * params[layer, 3, :, cols]).astype(BF16)
                place = BLOCK + STARTS[c]
                smooth[layer * nx + j, :, place:place + WIDES[c]] = smoothed
                if c == 0 and j == 0:
                    for k in range(nx):
                        smooth[layer * nx + k, :, :BLOCK] = smoothed[:, :BLOCK]
                inner = normed * (
                    0.7978845608028654 + 0.035677408136300125 * (normed * normed)
                )
                branch = 0.5 * normed * (1.0 + jnp.tanh(inner))
                updated = (current + params[layer, 2, :, cols] * branch).astype(BF16).astype(F32)
                hidden[:, cols] = updated
                new_total = new_total + fold_lanes(updated)
        return new_total

    lax.fori_loop(0, sections, layer_step, first_total)
    for c in range(CHUNKS):
        all_tok(lambda layer, to, c=c: tok_copy(c, layer, to, s, x).start())
    tokens[x * sections + s] = smooth[s * nx + x]
    drain(counts.at[:nx - 1], cnt_recv.at[0])

    group = nx * sections * rows

    def rsz(c, target, source):
        where = to_z(target)
        cols = quarter_cols(c)
        meta = pl.ds(0, 2 * BLOCK + WIDES[c])
        return (
            remote(part_z.at[target, :, cols], gram_z.at[source, :, cols], rsz_send.at[c],
                   rsz_recv.at[c], where),
            remote(mean_z_send.at[c, :, meta], mean_z.at[c, source, :, meta], rmz_send.at[c],
                   rmz_recv.at[c], where),
        )

    def along_z(c, target):
        cols = all_cols(c) if c in SWAPPED else own_cols(c, x)
        held = final.at[z, :, cols]
        return remote(held, held, agz_send.at[c], agz_recv.at[c], to_z(target))

    def along_x(c, target):
        cols = own_cols(c, x)
        held = final.at[z, :, cols] if c in SWAPPED else final.at[:, :, cols]
        return remote(held, held, agx_send.at[c], agx_recv.at[c], to_x(target))

    def near_copy(c, side):
        step = 1 if side == 0 else nx - 1
        held = final.at[:, :, own_cols(c, x)]
        return remote(held, held, near_send.at[c, side], near_recv.at[c, side],
                      to_x(lax.rem(x + step, nx)))

    def relay_copy(c, side):
        step = 1 if side == 0 else nx - 1
        origin = lax.rem(x + nx - step, nx)
        held = final.at[pl.ds(side * (nz // 2), nz // 2), :, own_cols(c, origin)]
        return remote(held, held, relay_send.at[c, side], relay_recv.at[c, side],
                      to_x(lax.rem(x + step, nx)))

    def drain_z(c, sem):
        size = nx * WIDES[c] if c in SWAPPED else WIDES[c]
        drain(final.at[:nz - 1, :, :size], sem.at[c])

    def drain_x(c, sem):
        size = (nx - 1) * WIDES[c]
        drain(final.at[0, :, :size] if c in SWAPPED else final.at[:, :, :size], sem.at[c])

    def agm(target, source):
        return remote(mean_part.at[source], mean_part.at[source], agm_send.at[0],
                      agm_recv.at[0], to_x(target))

    def start_both(pair):
        pair[0].start()
        pair[1].start()

    def gram_stage(c):
        drain(tokens.at[:nx * sections - 1, :, part_cols(c)], tok_recv.at[c])
        used = functools.reduce(jnp.add, [counts[k] for k in range(nx)]).astype(F32)
        if c == 0:
            place = lax.broadcasted_iota(jnp.int32, (sections * rows, BLOCK), 0)
            across = lax.broadcasted_iota(jnp.int32, (16, sections * rows), 1)
            valid = []
            for k in range(nx):
                here = counts[k][:, :1]
                valid.append((place < here).astype(F32).astype(BF16))
                valid_row[:, k * sections * rows:(k + 1) * sections * rows] = (
                    (across < here).astype(F32).astype(BF16)
                )
            valid = jnp.concatenate(valid, axis=0)
            block[...] = tokens[:, :, :BLOCK].reshape(group, BLOCK) * valid
            block_sum[...] = lax.dot_general(
                block[...], valid, CONTRACT_ROWS, preferred_element_type=F32
            )
        wide, start = WIDES[c], STARTS[c]
        here = tokens[:, :, BLOCK + start:BLOCK + start + wide].reshape(group, wide)
        mean_here = jnp.dot(valid_row[...], here, preferred_element_type=F32)[:1] / used[:, :1]
        if c == 0:
            first = tokens[:, :, :BLOCK].reshape(group, BLOCK)
            block_mean[...] = (
                jnp.dot(valid_row[...], first, preferred_element_type=F32)[:1] / used
            )
        moments = lax.dot_general(block[...], here, CONTRACT_ROWS, preferred_element_type=F32)
        moments = moments - block_sum[:, :1] * mean_here
        part_z[:, :, start:start + wide] = moments.astype(BF16).reshape(nz, slim, wide)
        mean_z_send[c, :, :BLOCK] = block_mean[...]
        mean_z_send[c, :, BLOCK:2 * BLOCK] = used
        mean_z_send[c, :, 2 * BLOCK:2 * BLOCK + wide] = mean_here
        others(nz, z, lambda k: start_both(rsz(c, k, z)))
        mean_z[c, z] = mean_z_send[c]
        gram_z[z, :, start:start + wide] = part_z[z, :, start:start + wide]

    def z_stage(c):
        wide, start = WIDES[c], STARTS[c]
        drain(mean_z.at[c, :nz - 1, :, :2 * BLOCK + wide], rmz_recv.at[c])
        drain(gram_z.at[:nz - 1, :, :wide], rsz_recv.at[c])
        joined, middle = merge_means(mean_z.at[c], nz, wide, spread)
        total = spread[pl.ds(pl.multiple_of(z * slim, slim), slim), :wide]
        for k in range(nz):
            total = total + gram_z[k, :, start:start + wide].astype(F32)
        final[z, :, own_cols(c, x)] = (total / joined).astype(BF16)
        mean_part[x, :, start:start + wide] = middle
        if c in SWAPPED:
            others(nx, x, lambda k: along_x(c, k).start())
        else:
            others(nz, z, lambda k: along_z(c, k).start())
        if c == CHUNKS - 1:
            others(nx, x, lambda k: agm(k, x).start())

    def a_stage(c):
        if c in SWAPPED:
            drain_x(c, agx_recv)
            others(nz, z, lambda k: along_z(c, k).start())
        else:
            drain_z(c, agz_recv)
            if c < RELAY:
                near_copy(c, 0).start()
                near_copy(c, 1).start()
            else:
                others(nx, x, lambda k: along_x(c, k).start())

    def b_stage(c):
        if c < RELAY:
            for side in range(2):
                near_copy(c, side).wait_recv()
                relay_copy(c, side).start()
        elif c in SWAPPED:
            drain_z(c, agz_recv)
        else:
            drain_x(c, agx_recv)

    def c_stage(c):
        if c < RELAY:
            relay_copy(c, 0).wait_recv()
            relay_copy(c, 1).wait_recv()

    stages = (gram_stage, z_stage, a_stage, b_stage, c_stage)
    for tick in range(CHUNKS + len(stages) - 1):
        for place, stage in enumerate(stages):
            if 0 <= tick - place < CHUNKS:
                stage(tick - place)

    drain(mean_part.at[:nx - 1], agm_recv.at[0])
    for k in range(nx):
        for c in range(CHUNKS):
            start, wide = STARTS[c], WIDES[c]
            place = nx * start + k * wide
            mean_full[:, place:place + wide] = mean_part[k, :, start:start + wide]

    others(ny, y, lambda k: params_across(k).wait_send())
    params_over().wait_send()
    others(ny, y, lambda k: params_on(2 * k + core).wait_send())
    drain(mean_part.at[:nx - 1], agm_send.at[0])

    drain(counts.at[:nx - 1], cnt_send.at[0])

    for c in range(CHUNKS):
        drain(smooth.at[:nx * sections - 1, :, part_cols(c)], tok_send.at[c])
        drain(part_z.at[:nz - 1, :, :WIDES[c]], rsz_send.at[c])
        drain(mean_z.at[c, :nz - 1, :, :2 * BLOCK + WIDES[c]], rmz_send.at[c])
        drain_z(c, agz_send)
        if c < RELAY:
            for side in range(2):
                near_copy(c, side).wait_send()
                relay_copy(c, side).wait_send()
        else:
            drain_x(c, agx_send)


def body(
    patches, patch_ids, pos_table, token_counts, norm_gain, norm_bias, branch_scale, act_range,
    weight_range, alpha_index,
):
    sections = lax.axis_size("section")
    toks = lax.axis_size("tok")
    nx, nz = RING_X, toks // RING_X
    width = patches.shape[1]
    rows = patches.shape[0] // sections
    quarter = width // nx
    slim = BLOCK // nz
    widest = max(WIDES)
    meta = widest + 2 * BLOCK
    dma = pltpu.SemaphoreType.DMA
    smem = pl.BlockSpec(memory_space=pltpu.SMEM)
    hbm = pl.BlockSpec(memory_space=pltpu.HBM)
    on_chip = pl.BlockSpec(memory_space=pltpu.VMEM)
    vmem = pltpu.VMEM
    each = dma((CHUNKS,))
    pair = dma((CHUNKS, 2))
    group = nx * sections * rows
    cov, mean = pl.pallas_call(
        functools.partial(kernel, sections, toks),
        out_shape=(
            pltpu.VMEM((nz, slim, width), BF16),
            pltpu.VMEM((1, width), F32),
        ),
        in_specs=[smem] * 3 + [hbm] * 7,
        out_specs=(on_chip, on_chip),
        scratch_shapes=[
            vmem((rows, width), BF16),
            vmem(pos_table.shape, BF16),
            vmem((2, 1, width), F32),
            vmem((sections, 4, 1, width), F32),
            vmem((rows, width), F32),
            vmem((sections * nx, rows, BLOCK + quarter), BF16),
            vmem((nx * sections, rows, BLOCK + quarter), BF16),
            vmem((nx, 1, 128), jnp.int32),
            vmem((16, group), BF16),
            vmem((group, BLOCK), BF16),
            vmem((BLOCK, BLOCK), F32),
            vmem((1, BLOCK), F32),
            vmem((nz, slim, quarter), BF16),
            vmem((CHUNKS, 1, meta), F32),
            vmem((nz, slim, quarter), BF16),
            vmem((CHUNKS, nz, 1, meta), F32),
            vmem((BLOCK, widest), F32),
            vmem((nx, 1, quarter), F32),
            dma((7,)),
            dma((sections // 2,)),
            dma((sections // 2,)),
            dma((sections,)),
            dma((1,)),
            dma((1,)),
            each, each,
            each, each, each, each,
            each, each,
            each, each,
            pair, pair, pair, pair,
            dma((1,)),
            dma((1,)),
        ],
        compiler_params=pltpu.CompilerParams(
            collective_id=0, has_side_effects=True, vmem_limit_bytes=58 * 1024 * 1024
        ),
        name="moments",
    )(
        patch_ids, token_counts, alpha_index, patches, pos_table, norm_gain, norm_bias,
        branch_scale, act_range, weight_range,
    )
    return cov.reshape(1, BLOCK, width).astype(F32), mean


def solution(mesh):
    in_specs = (
        P("tok", None),
        P("tok"),
        P(),
        P("tok"),
        P("section", None),
        P("section", None),
        P("section", None),
        P("section", None),
        P("section", None),
        P("section"),
    )
    out_specs = (P("section", None, None), P("section", None))
    return jax.shard_map(body, mesh=mesh, in_specs=in_specs, out_specs=out_specs, check_vma=False)
```
